128 devices in a mesh: ctx: 16 (over x, z), exp: 8 (over y, core).
Axes of the slice: x: 4, y: 4, z: 4, core: 2. Of those that a mesh axis runs over, the one named last changes fastest.
Arguments:
- residual: bfloat16 [16384, 6400], P(('ctx', 'exp')), may hold values from -6 to 6
- shared_out: bfloat16 [16384, 6400], P(('ctx', 'exp')), may hold values from -6 to 6
- expert_out: bfloat16 [16, 8, 8, 2, 16, 6400], P('ctx', 'exp'), may hold values from -6 to 6
- expert_id: int32 [16384, 1], P(('ctx', 'exp')), may hold values from 0 to 15; in each aligned block of 128 rows (0 to 127, 128 to 255, ...) at most 16 rows name the same one
- gate_value: float32 [16384, 1], P(('ctx', 'exp')), may hold values from 0.3 to 1
- doc_lengths: int32 [32], replicated, may hold values from 1 to 2049, 16384 in all
- norm_gain: float32 [6400], replicated, may hold values from 0.1 to 1.9
- w_query: bfloat16 [6400, 5120], P('ctx', 'exp'), may hold values from -0.078125 to 0.078125
- key_value_weight: bfloat16 [6400, 1024], P('ctx'), may hold values from -0.078125 to 0.078125
- query_gain: float32 [128], replicated, may hold values from 0.5 to 24
- key_gain: float32 [128], replicated, may hold values from 0.5 to 24
Outputs:
- hidden_out: bfloat16 [16384, 6400], P(('ctx', 'exp'))
- attended: bfloat16 [16384, 5120], P('ctx', 'exp')
The draws below stay inside these ranges and needn't reach their ends.
Inputs may be any that keep to these rules, and one draw needn't show every extreme that they name: `expert_id`: in the rows of one device no expert is named by more than 16 tokens, and some expert by exactly that many. `doc_lengths`: the lengths sum to 16384; the longest is 2049.
All inputs are finite; a program needn't handle non-finite values.
Results may differ from the reference program's by a relative error of at most 0.017.
The reference program's roundings to bfloat16 on the way (of `routed_rows`, `normed`, `queries`, `key_rows`, `value_rows` and `probs`) count: a program that leaves them out, or rounds other values in their place, can miss the bound.
Values may be sent and summed in bfloat16 or wider, within the bound.
A program may use at most 192 MiB of HBM per device.

```python
import math
import jax
import jax.numpy as jnp
import numpy as np
from jax import lax

MODEL_DIM = 6400
HEAD_DIM = 128
QUERY_HEADS = 40
KEY_VALUE_HEADS = 4
EXPERTS = 16
DOC_SHARD_SPAN = 2
TOK_DEV = 128
SHARD_TOKENS = 1024
PACKED_TOKENS = 16384
DOC_MOST = 2049
NDOC = 32
ROUTE_MOST = 16
E_DEV = 2
N_CTX = 16
N_EXP = 8


def picked_channels(key):
    return jax.random.randint(key, (2,), 0, HEAD_DIM)


def spread_gain(key, channels, largest):
    spread = jnp.exp(jax.random.uniform(key, (HEAD_DIM,), jnp.float32, math.log(0.5), math.log(2.0)))
    chosen = jnp.any(jnp.arange(HEAD_DIM)[:, None] == channels[None, :], axis=1)
    return jnp.where(chosen, jnp.maximum(spread, largest), spread)


def draw_query_gain(key, part):
    channels = picked_channels(key)
    key = jax.random.fold_in(key, 17)
    largest = 1.0
    return spread_gain(key, channels, largest)


def draw_key_gain(key, part):
    channels = picked_channels(key)
    key = jax.random.fold_in(key, 29)
    largest = 1.0
    return spread_gain(key, channels, largest)


def steps_of(stream_key, extent, pieces, least, high):
    level, own = 1.0, jax.random.fold_in(stream_key, 6)
    for position, parts in pieces:
        steps = jnp.exp(jax.random.uniform(jax.random.fold_in(own, position), (parts,), jnp.float32, least / len(pieces), high / len(pieces)))
        level = level * jnp.repeat(steps, extent[position] // parts).reshape([-1 if axis == position else 1 for axis in range(len(extent))])
    return level


def split_up(number_of, total, bound, slope):
    portions = [(1 << 20) // math.isqrt(standing ** slope) + 1 for standing in range(2, number_of + 1)]
    rest, holding = total - bound - (number_of - 1), [1] * (number_of - 1)
    while rest > 0:
        candidates = [i for i in range(number_of - 1) if holding[i] < bound]
        pool, budget = sum([portions[i] for i in candidates]), rest
        for i in candidates:
            extra = min(bound - holding[i], max(1, budget * portions[i] // pool), rest)
            holding[i] = holding[i] + extra
            rest = rest - extra
    return np.array([bound] + holding)


def ragged_sizes(stream_key, amount, total, limit, slope):
    if amount == 2:
        one = jax.random.randint(stream_key, (), max(1, total - limit), min(limit, total - 1) + 1)
        return jnp.stack([one, total - one])
    sizes = jnp.asarray(split_up(amount, total, limit, slope), jnp.int32)
    twos = (amount - 1) // 2
    giver, receiver = sizes[1:1 + 2 * twos:2], sizes[2:2 + 2 * twos:2]
    margin = jnp.minimum(giver - 1, limit - receiver)
    shifted = jax.random.randint(jax.random.fold_in(stream_key, 1), (twos,), 0, 1 << 20) % (margin + 1)
    sizes = sizes.at[1:1 + 2 * twos:2].set(giver - shifted).at[2:2 + 2 * twos:2].set(receiver + shifted)
    return sizes[jax.random.permutation(jax.random.fold_in(stream_key, 2), amount)]


def routed_block(own_key, own, number, rows, number_of, top, limit, skew):
    sequence = jax.random.permutation(own_key, number_of)
    crowded, common = shares(number_of, rows * top, limit, skew, True), shares(number_of, rows * top, limit, skew, False)
    places = jnp.arange(number_of)

    def named(lengths, turn):
        used = int((lengths > 0).sum())
        fixed = max(1, used // 4)
        passed = fixed + (places - fixed + turn * (used - fixed)) % max(1, number_of - fixed)
        return jnp.zeros((number_of,), jnp.int32).at[sequence[jnp.where(places < fixed, places, passed)]].set(jnp.asarray(lengths, jnp.int32))

    lengths = jnp.where(number % 4 == 0, named(crowded, number // 4), named(common, number - number // 4 - 1))
    mixed = jax.random.permutation(jax.random.fold_in(own, 3), number_of)
    source_of, receiver = mixed[0:number_of // 2 * 2:2], mixed[1:number_of // 2 * 2:2]
    slack = jnp.minimum(lengths[source_of] - 1, limit - lengths[receiver]) // 2
    slack = jnp.where((source_of == sequence[0]) | (receiver == sequence[0]) | (lengths[receiver] == 0), 0, jnp.maximum(slack, 0))
    passed = jax.random.randint(jax.random.fold_in(own, 4), (number_of // 2,), 0, 1 << 20) % (slack + 1)
    lengths = lengths.at[source_of].add(-passed).at[receiver].add(passed)
    items = jnp.searchsorted(jnp.cumsum(lengths), jnp.arange(rows * top), side="right").astype(jnp.int32)
    table = items.reshape(top, rows).T
    table = table[jax.random.permutation(jax.random.fold_in(own, 1), rows)]
    turn = jax.random.randint(jax.random.fold_in(own, 2), (rows, 1), 0, top)
    return jnp.take_along_axis(table, (jnp.arange(top)[None, :] + turn) % top, axis=1)


def shares(amount, total, limit, lean, full):
    portions = [(1 << 20) // math.isqrt(grade ** lean) + 1 for grade in range(1, amount + 1)]
    largest = limit if full else min(limit, max(-(-total // amount), total * portions[0] // sum(portions)))
    least = 1 if total - largest >= amount - 1 else 0
    holding, rest = [largest] + [least] * (amount - 1), total - largest - least * (amount - 1)
    while rest > 0:
        candidates = [i for i in range(1, amount) if holding[i] < largest] or [i for i in range(1, amount) if holding[i] < limit]
        pool, remaining = sum([portions[i] for i in candidates]), rest
        for i in candidates:
            extra = min(limit - holding[i], max(1, remaining * portions[i] // pool), rest)
            holding[i] = holding[i] + extra
            rest = rest - extra
    return np.array(holding)


def normal_values(key, dims, width, most, shards=(), kind=jnp.bfloat16):
    values = width * jax.random.normal(key, dims, jnp.float32)
    if shards:
        values = values * steps_of(key, dims, shards, -0.22, 0.18)
    return jnp.clip(values, -most, most).astype(kind)


def setup_inputs(seed: int = 0) -> dict:
    splits = jax.random.split(jax.random.key(seed), 12)
    residual = normal_values(splits[0], (PACKED_TOKENS, MODEL_DIM), 1.0, 6.0, ((0, 128),))
    shared_out = normal_values(splits[1], (PACKED_TOKENS, MODEL_DIM), 0.7, 6.0, ((0, 128),))
    expert_out = normal_values(splits[2], (N_CTX, N_EXP, N_EXP, E_DEV, ROUTE_MOST, MODEL_DIM), 1.0, 6.0, ((0, 16), (1, 8)))
    expert_id_keys = jax.random.split(jax.random.fold_in(splits[3], 1), PACKED_TOKENS // TOK_DEV)
    expert_id_turns = jax.random.permutation(jax.random.fold_in(splits[3], 3), PACKED_TOKENS // TOK_DEV)
    expert_id = jax.vmap(lambda own, number: routed_block(jax.random.fold_in(splits[3], 2), own, number, TOK_DEV, EXPERTS, 1, ROUTE_MOST, 2))(expert_id_keys, expert_id_turns).reshape((PACKED_TOKENS, 1))
    gate_value = jnp.clip(0.3 + 0.7 * jax.random.uniform(splits[4], (PACKED_TOKENS, 1), jnp.float32) ** steps_of(splits[4], (PACKED_TOKENS, 1), ((0, 128),), -0.2, 0.2), 0.3, 1.0)
    doc_lengths = ragged_sizes(splits[5], NDOC, PACKED_TOKENS, DOC_MOST, 2).astype(jnp.int32)
    norm_gain = jnp.clip(1.0 + 0.18 * jax.random.normal(splits[6], (MODEL_DIM,), jnp.float32), 0.1, 1.9)
    w_query = normal_values(splits[7], (MODEL_DIM, QUERY_HEADS * HEAD_DIM), MODEL_DIM ** -0.5, 0.078125, ((0, 16), (1, 8)))
    key_value_weight = normal_values(splits[8], (MODEL_DIM, KEY_VALUE_HEADS * 2 * HEAD_DIM), MODEL_DIM ** -0.5, 0.078125, ((0, 16),))
    query_gain = draw_query_gain(jax.random.fold_in(splits[11], 71), 0)
    key_gain = draw_key_gain(jax.random.fold_in(splits[11], 71), 0)
    return {"residual": residual, "shared_out": shared_out, "expert_out": expert_out, "expert_id": expert_id, "gate_value": gate_value, "doc_lengths": doc_lengths, "norm_gain": norm_gain, "w_query": w_query, "key_value_weight": key_value_weight, "query_gain": query_gain, "key_gain": key_gain}


eps_value = 1e-06
neg_large = -1e+30

def rms_scale(values_in, gain_vector):
    mean_square = lax.optimization_barrier(jnp.mean(values_in * values_in, axis=-1, keepdims=True))
    return values_in * lax.rsqrt(mean_square + eps_value) * gain_vector

def document_of(positions, doc_lengths):
    doc_ends = jnp.cumsum(doc_lengths)
    return lax.optimization_barrier(jnp.sum((doc_ends[None, :] <= positions[:, None]).astype(jnp.int32), axis=1))

def reference(residual, shared_out, expert_out, expert_id, gate_value, doc_lengths, norm_gain, w_query, key_value_weight, query_gain, key_gain):
    device_count = N_CTX * N_EXP
    chosen = expert_id[:, 0].reshape(device_count, TOK_DEV)
    onehot = (chosen[..., None] == jnp.arange(EXPERTS, dtype=jnp.int32)[None, None, :]).astype(jnp.int32)
    before = jnp.cumsum(onehot, axis=1) - onehot
    slot_index = lax.optimization_barrier(jnp.sum(onehot * before, axis=2))
    device_ids = jnp.arange(device_count, dtype=jnp.int32)[:, None] + jnp.zeros((1, TOK_DEV), jnp.int32)
    ctx_ids = device_ids // N_EXP
    source_ids = device_ids % N_EXP
    holder_ids = chosen // E_DEV
    local_ids = chosen % E_DEV
    routed_rows = expert_out[ctx_ids, holder_ids, source_ids, local_ids, slot_index].reshape(PACKED_TOKENS, MODEL_DIM)
    summed = residual.astype(jnp.float32) + shared_out.astype(jnp.float32) + gate_value * routed_rows.astype(jnp.float32)
    hidden_out = summed.astype(jnp.bfloat16)
    normed = rms_scale(summed, norm_gain).astype(jnp.bfloat16)
    query_raw = jnp.dot(normed, w_query, preferred_element_type=jnp.float32)
    key_value_projected = jnp.dot(normed, key_value_weight, preferred_element_type=jnp.float32)
    queries = rms_scale(query_raw.reshape(PACKED_TOKENS, QUERY_HEADS, HEAD_DIM), query_gain).astype(jnp.bfloat16)
    separate_key_value = key_value_projected.reshape(PACKED_TOKENS, KEY_VALUE_HEADS, 2, HEAD_DIM)
    key_rows = rms_scale(separate_key_value[:, :, 0, :], key_gain).astype(jnp.bfloat16)
    value_rows = separate_key_value[:, :, 1, :].astype(jnp.bfloat16)
    leading_part = jnp.zeros((DOC_SHARD_SPAN * SHARD_TOKENS, KEY_VALUE_HEADS, HEAD_DIM), jnp.bfloat16)
    key_padded = jnp.concatenate([leading_part, key_rows], axis=0)
    value_padded = jnp.concatenate([leading_part, value_rows], axis=0)
    query_group_count = QUERY_HEADS // KEY_VALUE_HEADS
    score_scale = HEAD_DIM ** (-0.5)
    window = (DOC_SHARD_SPAN + 1) * SHARD_TOKENS

    def one_shard(shard_index):
        start_row = (shard_index * SHARD_TOKENS).astype(jnp.int32)
        query_pos = start_row + jnp.arange(SHARD_TOKENS, dtype=jnp.int32)
        key_pos = start_row - DOC_SHARD_SPAN * SHARD_TOKENS + jnp.arange(window, dtype=jnp.int32)
        query_doc = document_of(query_pos, doc_lengths)
        key_doc = document_of(key_pos, doc_lengths)
        allowed = (key_doc[None, :] == query_doc[:, None]) & (key_pos[None, :] <= query_pos[:, None]) & (key_pos[None, :] >= 0)
        shard_queries = lax.dynamic_slice_in_dim(queries, start_row, SHARD_TOKENS, 0)
        shard_keys = lax.dynamic_slice_in_dim(key_padded, start_row, window, 0)
        shard_values = lax.dynamic_slice_in_dim(value_padded, start_row, window, 0)

        def one_head(head_index):
            kv_index = (head_index // query_group_count).astype(jnp.int32)
            head_query = lax.dynamic_index_in_dim(shard_queries, head_index, 1, keepdims=False).astype(jnp.float32)
            head_key = lax.dynamic_index_in_dim(shard_keys, kv_index, 1, keepdims=False).astype(jnp.float32)
            head_value = lax.dynamic_index_in_dim(shard_values, kv_index, 1, keepdims=False)
            scores = jnp.dot(head_query, head_key.T, precision=lax.Precision.HIGHEST) * score_scale
            scores = jnp.where(allowed, scores, neg_large)
            row_max = lax.optimization_barrier(jnp.max(scores, axis=1, keepdims=True))
            weights_now = jnp.where(allowed, jnp.exp(scores - row_max), 0.0)
            total = lax.optimization_barrier(jnp.sum(weights_now, axis=1, keepdims=True))
            probs = weights_now.astype(jnp.bfloat16)
            mixed = jnp.dot(probs, head_value, preferred_element_type=jnp.float32)
            return mixed / total
        per_head = lax.map(one_head, jnp.arange(QUERY_HEADS, dtype=jnp.int32))
        return jnp.transpose(per_head, (1, 0, 2)).reshape(SHARD_TOKENS, QUERY_HEADS * HEAD_DIM)
    attended = lax.map(one_shard, jnp.arange(N_CTX, dtype=jnp.int32)).reshape(PACKED_TOKENS, QUERY_HEADS * HEAD_DIM).astype(jnp.bfloat16)
    return (hidden_out, attended)
```

```python
import functools
import math

import jax
import jax.numpy as jnp
from jax import lax
from jax.experimental import pallas as pl
from jax.experimental.pallas import tpu as pltpu
from jax.sharding import PartitionSpec as P

MESH = pl.DeviceIdType.MESH
MODEL = 6400
HEAD = 128
HEADS = 5
COLS = (HEADS + 1) * HEAD
TOK = 128
SHARD = 1024
N_CTX = 16
N_EXP = 8
SLOTS = 32
FCH = 5
FW = MODEL // FCH
PCH = 4
PR = TOK // PCH
PM = N_EXP * PR
WROWS = 400
WA = 208
WB = WROWS - WA
EPS = 1e-06
VMEM_LIMIT = 56 * 1024 * 1024


def rms_rows(values, gain):
    mean_square = jnp.mean(values * values, axis=-1, keepdims=True)
    return values * lax.rsqrt(mean_square + EPS) * gain


def exchange_kernel(
    res_hbm, sh_hbm, ex_hbm, eid_ref, gate_ref, gain_ref, wq_hbm, wkv_hbm, qg_ref, kg_ref,
    hid_hbm, q_hbm, kv_hbm,
    slots, res, sh, summed, hid, xall, wall, qbuf, kvbuf,
    loc_sem, a_send, a_recv, a_own, w_send, w_recv1, w_recv2, x_send, x_recv, s_send, s_recv,
    h_send, h_recv, hs_send, hs_recv, out_sem,
):
    c = lax.axis_index("ctx")
    e = lax.axis_index("exp")
    x, z = c // 4, c % 4
    y, k = e // 2, e % 2

    def along_x(d):
        return (((x + d) % 4) * 4 + z, e)

    def along_z(d):
        return (x * 4 + (z + d) % 4, e)

    def along_y(d):
        return (c, ((y + d) % 4) * 2 + k)

    def along_ctx(d):
        return ((c + d + N_CTX) % N_CTX, e)

    sibling = (c, y * 2 + (1 - k))

    def remote(src, dst, send, recv, to):
        pltpu.make_async_remote_copy(
            src_ref=src, dst_ref=dst, send_sem=send, recv_sem=recv, device_id=to, device_id_type=MESH
        ).start()

    def done(ref, sem):
        pltpu.make_async_copy(ref, ref, sem).wait()

    w_own = wall.at[pl.ds(pl.multiple_of(c * WROWS, 16), WROWS), :]
    load_q = pltpu.make_async_copy(wq_hbm, w_own.at[:, : HEADS * HEAD], loc_sem.at[0])
    load_q.start()
    kv_column = pl.multiple_of(e * HEAD, HEAD)
    load_kv = pltpu.make_async_copy(
        wkv_hbm.at[:, pl.ds(kv_column, HEAD)], w_own.at[:, HEADS * HEAD :], loc_sem.at[1]
    )
    load_kv.start()
    load_res = pltpu.make_async_copy(res_hbm, res, loc_sem.at[2])
    load_res.start()
    load_sh = pltpu.make_async_copy(sh_hbm, sh, loc_sem.at[3])
    load_sh.start()
    mine = pl.ds(pl.multiple_of(e * SLOTS, SLOTS), SLOTS)
    for f in range(FCH):
        pltpu.make_async_copy(
            ex_hbm.at[e, :, pl.ds(f * FW, FW)], slots.at[f, mine, :], a_own.at[f]
        ).start()

    barrier = pltpu.get_barrier_semaphore()
    for d in range(1, N_EXP):
        pl.semaphore_signal(barrier, inc=1, device_id=(c, (e + d) % N_EXP), device_id_type=MESH)
    for d in range(1, 4):
        pl.semaphore_signal(barrier, inc=1, device_id=along_x(d), device_id_type=MESH)
        pl.semaphore_signal(barrier, inc=1, device_id=along_z(d), device_id_type=MESH)
    for d in (-2, -1, 1, 2):
        pl.semaphore_signal(barrier, inc=1, device_id=along_ctx(d), device_id_type=MESH)
    pl.semaphore_wait(barrier, (N_EXP - 1) + 6 + 4)

    @pl.loop(0, FCH)
    def _(f):
        columns = pl.ds(pl.multiple_of(f * FW, 128), FW)
        for d in range(1, N_EXP):
            to = (e + d) % N_EXP
            remote(ex_hbm.at[to, :, columns], slots.at[f, mine, :], a_send, a_recv.at[f], (c, to))

    def half_a(index):
        return wall.at[pl.ds(pl.multiple_of(index * WROWS, 16), WA), :]

    def half_b(index):
        return wall.at[pl.ds(pl.multiple_of(index * WROWS + WA, 16), WB), :]

    load_q.wait()
    load_kv.wait()
    for d in (1, 3, 2):
        remote(half_a(c), half_a(c), w_send.at[0], w_recv1.at[0, d], along_x(d))
        remote(half_b(c), half_b(c), w_send.at[1], w_recv1.at[1, d], along_z(d))
    for d in (1, 3, 2):
        remote(half_a(c), half_a(c), w_send.at[0], w_recv2.at[0], along_z(d))
        remote(half_b(c), half_b(c), w_send.at[1], w_recv2.at[1], along_x(d))

    experts = 2 * N_EXP
    chosen = eid_ref[...]
    named = chosen == lax.broadcasted_iota(jnp.int32, (TOK, experts), 1)
    named = jnp.where(named, 1.0, 0.0)
    earlier = lax.broadcasted_iota(jnp.int32, (TOK, TOK), 1) < lax.broadcasted_iota(
        jnp.int32, (TOK, TOK), 0
    )
    before = jnp.dot(
        jnp.where(earlier, 1.0, 0.0).astype(jnp.bfloat16),
        named.astype(jnp.bfloat16),
        preferred_element_type=jnp.float32,
    )
    slot = jnp.sum(named * before, axis=1, keepdims=True)
    row = chosen.astype(jnp.float32) * float(SLOTS // 2) + slot
    lane = lax.broadcasted_iota(jnp.int32, (TOK, N_EXP * SLOTS), 1).astype(jnp.float32)
    pick = jnp.where(lane == row, 1.0, 0.0).astype(jnp.bfloat16)
    gate = gate_ref[...]

    for d in (1, 3, 2):
        done(half_a(0), w_recv1.at[0, d])
        got = ((x - d + 4) % 4) * 4 + z
        for d2 in (1, 3, 2):
            remote(half_a(got), half_a(got), w_send.at[0], w_recv2.at[0], along_z(d2))
        done(half_b(0), w_recv1.at[1, d])
        got = x * 4 + (z - d + 4) % 4
        for d2 in (1, 3, 2):
            remote(half_b(got), half_b(got), w_send.at[1], w_recv2.at[1], along_x(d2))

    load_res.wait()
    load_sh.wait()
    squares = jnp.zeros((TOK, 1), jnp.float32)
    for f in range(FCH):
        done(slots.at[f, pl.ds(0, SLOTS), :], a_own.at[f])
        done(slots.at[f, pl.ds(0, SLOTS * (N_EXP - 1)), :], a_recv.at[f])
        columns = pl.ds(f * FW, FW)
        routed = jnp.dot(pick, slots[f], preferred_element_type=jnp.float32)
        total = (
            res[:, columns].astype(jnp.float32) + sh[:, columns].astype(jnp.float32) + gate * routed
        )
        hid[:, columns] = total.astype(jnp.bfloat16)
        summed[:, columns] = total
        squares = squares + jnp.sum(total * total, axis=1, keepdims=True)
    scale = lax.rsqrt(squares * (1.0 / MODEL) + EPS)
    here = pl.ds(pl.multiple_of(e * PR, PR), PR)
    gain = gain_ref[...]
    for p in range(PCH):
        rows = slice(p * PR, (p + 1) * PR)
        xall[p, here, :] = (summed[rows, :] * scale[rows] * gain).astype(jnp.bfloat16)
        block = xall.at[p, here, :]
        for d in (1, 3, 2):
            remote(block, block, x_send, x_recv.at[p, d], along_y(d))
        remote(block, block, s_send, s_recv.at[p], sibling)
    store_hid = pltpu.make_async_copy(hid, hid_hbm, out_sem.at[0])
    store_hid.start()

    done(wall.at[pl.ds(0, 12 * WA), :], w_recv2.at[0])
    done(wall.at[pl.ds(0, 12 * WB), :], w_recv2.at[1])

    def pass_halo(p):
        for dist in (1, 2):
            part = kv_hbm.at[2 - dist, k, :, p]
            done(part, h_recv.at[p, dist])
            remote(part, part, hs_send, hs_recv, sibling)

    @pl.loop(0, PCH)
    def _(p):
        for d in (1, 3, 2):
            source = ((y - d + 4) % 4) * 2 + k
            block = xall.at[p, pl.ds(pl.multiple_of(source * PR, PR), PR), :]
            done(block, x_recv.at[p, d])
            remote(block, block, s_send, s_recv.at[p], sibling)
        done(xall.at[p, pl.ds(0, 4 * PR), :], s_recv.at[p])

        last = jnp.dot(
            xall[p], wall[:, (HEADS - 1) * HEAD :], preferred_element_type=jnp.float32
        )
        raw = last[:, HEAD:]
        part = jnp.where(k == 0, rms_rows(raw, kg_ref[...]), raw).astype(jnp.bfloat16)
        kvbuf[p] = part.reshape(N_EXP, PR, HEAD)
        for dist in (1, 2):
            remote(
                kvbuf.at[p], kv_hbm.at[2 - dist, k, :, p], h_send, h_recv.at[p, dist], along_ctx(dist)
            )
        remote(kvbuf.at[p], kv_hbm.at[2, k, :, p], hs_send, hs_recv, sibling)
        pltpu.make_async_copy(kvbuf.at[p], kv_hbm.at[2, k, :, p], out_sem.at[1]).start()
        head = rms_rows(last[:, :HEAD], qg_ref[...]).astype(jnp.bfloat16)
        qbuf[p, :, :, (HEADS - 1) * HEAD :] = head.reshape(N_EXP, PR, HEAD)
        for pair in range((HEADS - 1) // 2):
            low = pair * 2 * HEAD
            raw = jnp.dot(
                xall[p], wall[:, low : low + 2 * HEAD], preferred_element_type=jnp.float32
            )
            for i in range(2):
                head = rms_rows(raw[:, i * HEAD : (i + 1) * HEAD], qg_ref[...]).astype(jnp.bfloat16)
                qbuf[p, :, :, low + i * HEAD : low + (i + 1) * HEAD] = head.reshape(N_EXP, PR, HEAD)
        pltpu.make_async_copy(qbuf.at[p], q_hbm.at[:, p], out_sem.at[2]).start()

        @pl.when(p > 0)
        def _():
            pass_halo(p - 1)

    pass_halo(PCH - 1)

    done(ex_hbm.at[pl.ds(0, N_EXP - 1)], a_send)
    done(wall.at[pl.ds(0, 15 * WA), :], w_send.at[0])
    done(wall.at[pl.ds(0, 15 * WB), :], w_send.at[1])
    done(xall.at[:, pl.ds(0, 3 * PR), :], x_send)
    done(xall.at[:, pl.ds(0, 4 * PR), :], s_send)
    done(kv_hbm.at[pl.ds(0, 2), 0], h_send)
    done(kv_hbm.at[:, 0], hs_send)
    done(kv_hbm.at[:, 0], hs_recv)
    store_hid.wait()
    done(kv_hbm.at[0, 0], out_sem.at[1])
    done(q_hbm, out_sem.at[2])


def exchange(residual, shared_out, expert_rows, expert_id, gate, gain, w_query, w_kv, q_gain, k_gain):
    any_space = pl.BlockSpec(memory_space=pl.ANY)
    vmem = pl.BlockSpec(memory_space=pltpu.VMEM)
    dma = pltpu.SemaphoreType.DMA
    bf16, f32 = jnp.bfloat16, jnp.float32
    return pl.pallas_call(
        exchange_kernel,
        out_shape=(
            jax.ShapeDtypeStruct((TOK, MODEL), bf16),
            jax.ShapeDtypeStruct((N_EXP, PCH, PR, HEADS * HEAD), bf16),
            jax.ShapeDtypeStruct((3, 2, N_EXP, PCH, PR, HEAD), bf16),
        ),
        in_specs=[any_space] * 3 + [vmem] * 3 + [any_space] * 2 + [vmem] * 2,
        out_specs=(any_space, any_space, any_space),
        scratch_shapes=[
            pltpu.VMEM((FCH, N_EXP * SLOTS, FW), bf16),
            pltpu.VMEM((TOK, MODEL), bf16),
            pltpu.VMEM((TOK, MODEL), bf16),
            pltpu.VMEM((TOK, MODEL), f32),
            pltpu.VMEM((TOK, MODEL), bf16),
            pltpu.VMEM((PCH, PM, MODEL), bf16),
            pltpu.VMEM((MODEL, COLS), bf16),
            pltpu.VMEM((PCH, N_EXP, PR, HEADS * HEAD), bf16),
            pltpu.VMEM((PCH, N_EXP, PR, HEAD), bf16),
            dma((4,)),
            dma,
            dma((FCH,)),
            dma((FCH,)),
            dma((2,)),
            dma((2, 4)),
            dma((2,)),
            dma,
            dma((PCH, 4)),
            dma,
            dma((PCH,)),
            dma,
            dma((PCH, 3)),
            dma,
            dma,
            dma((3,)),
        ],
        compiler_params=pltpu.CompilerParams(
            collective_id=0, has_side_effects=True, vmem_limit_bytes=VMEM_LIMIT
        ),
        cost_estimate=pl.CostEstimate(
            flops=2 * SHARD * MODEL * COLS, bytes_accessed=16 * 1024 * 1024, transcendentals=0
        ),
        name="exchange",
    )(residual, shared_out, expert_rows, expert_id, gate, gain, w_query, w_kv, q_gain, k_gain)


BQ = 256
BK = 256
NEG = -1e30
LOG2E = math.log2(math.e)


def attention_kernel(
    doc_ref, q_ref, kv_ref, hid_hbm, out_ref, hid_out_hbm, vt, m_ref, l_ref, acc_ref, sem
):
    c = lax.axis_index("ctx")
    copy = pltpu.make_async_copy(hid_hbm, hid_out_hbm, sem)
    copy.start()
    window = c * SHARD - 2 * SHARD
    span = 3 * SHARD
    for part in range(3):
        vt[:, part * SHARD : (part + 1) * SHARD] = kv_ref[part, 1].T

    factor = HEAD ** (-0.5) * LOG2E

    @pl.loop(0, SHARD // BQ)
    def _(qb):
        q_low = 2 * SHARD + qb * BQ
        q_rows = pl.ds(pl.multiple_of(qb * BQ, BQ), BQ)
        position = q_low + lax.broadcasted_iota(jnp.int32, (1, BQ), 1)

        def starts(i, carried):
            end, first, least = carried
            end = end + doc_ref[i]
            first = jnp.where(end <= position, end, first)
            return end, first, jnp.where(end <= q_low, end, least)

        _, first, least = lax.fori_loop(
            0, doc_ref.shape[0], starts,
            (0 - window, jnp.zeros((1, BQ), jnp.int32) - window, 0 - window),
        )
        m_ref[...] = jnp.full(m_ref.shape, NEG, jnp.float32)
        l_ref[...] = jnp.zeros(l_ref.shape, jnp.float32)
        acc_ref[...] = jnp.zeros(acc_ref.shape, jnp.float32)

        def block(kb, carried):
            k_low = pl.multiple_of(kb * BK, BK)
            keys = kv_ref.at[kb // (SHARD // BK), 0][
                pl.ds(pl.multiple_of((kb % (SHARD // BK)) * BK, BK), BK), :
            ]
            values = vt[:, pl.ds(k_low, BK)]
            k_position = k_low + lax.broadcasted_iota(jnp.int32, (BK, 1), 0)
            allowed = (k_position >= first) & (k_position <= position)
            for h in range(HEADS):
                scores = lax.dot_general(
                    keys, q_ref[q_rows, h * HEAD : (h + 1) * HEAD], (((1,), (1,)), ((), ())),
                    preferred_element_type=jnp.float32,
                )
                scores = jnp.where(allowed, scores * factor, NEG)
                old = m_ref[h : h + 1, :]
                new = jnp.maximum(old, jnp.max(scores, axis=0, keepdims=True))
                weights = jnp.where(allowed, jnp.exp2(scores - new), 0.0)
                shrink = jnp.exp2(old - new)
                m_ref[h : h + 1, :] = new
                l_ref[h : h + 1, :] = l_ref[h : h + 1, :] * shrink + jnp.sum(
                    weights, axis=0, keepdims=True
                )
                acc_ref[h] = acc_ref[h] * shrink + jnp.dot(
                    values, weights.astype(jnp.bfloat16), preferred_element_type=jnp.float32
                )
            return carried

        lax.fori_loop(least // BK, (q_low + BQ) // BK, block, 0)
        for h in range(HEADS):
            finished = acc_ref[h] / l_ref[h : h + 1, :]
            out_ref[q_rows, h * HEAD : (h + 1) * HEAD] = finished.T.astype(jnp.bfloat16)

    copy.wait()


def attention(doc_lengths, queries, kv, hidden):
    vmem = pl.BlockSpec(memory_space=pltpu.VMEM)
    any_space = pl.BlockSpec(memory_space=pl.ANY)
    return pl.pallas_call(
        attention_kernel,
        out_shape=(
            jax.ShapeDtypeStruct((SHARD, HEADS * HEAD), jnp.bfloat16),
            jax.ShapeDtypeStruct((TOK, MODEL), jnp.bfloat16),
        ),
        in_specs=[pl.BlockSpec(memory_space=pltpu.SMEM), vmem, vmem, any_space],
        out_specs=(vmem, any_space),
        scratch_shapes=[
            pltpu.VMEM((HEAD, 3 * SHARD), jnp.bfloat16),
            pltpu.VMEM((8, BQ), jnp.float32),
            pltpu.VMEM((8, BQ), jnp.float32),
            pltpu.VMEM((HEADS, HEAD, BQ), jnp.float32),
            pltpu.SemaphoreType.DMA,
        ],
        compiler_params=pltpu.CompilerParams(vmem_limit_bytes=VMEM_LIMIT),
        name="attention",
    )(doc_lengths, queries, kv, hidden)


def per_device(
    residual, shared_out, expert_out, expert_id, gate_value, doc_lengths, norm_gain, w_query,
    key_value_weight, query_gain, key_gain,
):
    hidden, queries, kv = exchange(
        residual,
        shared_out,
        expert_out.reshape(N_EXP, SLOTS, MODEL),
        expert_id,
        gate_value,
        norm_gain.reshape(1, MODEL),
        w_query,
        key_value_weight,
        query_gain.reshape(1, HEAD),
        key_gain.reshape(1, HEAD),
    )
    attended, hidden_out = attention(
        doc_lengths, queries.reshape(SHARD, HEADS * HEAD), kv.reshape(3, 2, SHARD, HEAD), hidden
    )
    return (hidden_out, attended)


def solution(mesh):
    placed = (
        P(("ctx", "exp"), None),
        P(("ctx", "exp"), None),
        P("ctx", "exp", None, None, None, None),
        P(("ctx", "exp"), None),
        P(("ctx", "exp"), None),
        P(),
        P(),
        P("ctx", "exp"),
        P("ctx", None),
        P(),
        P(),
    )
    return jax.shard_map(
        per_device,
        mesh=mesh,
        in_specs=placed,
        out_specs=(P(("ctx", "exp"), None), P("ctx", "exp")),
        check_vma=False,
    )
```

```python
import functools
import math

import jax
import jax.numpy as jnp
from jax import lax
from jax.experimental import pallas as pl
from jax.experimental.pallas import tpu as pltpu
from jax.sharding import PartitionSpec as P

MESH = pl.DeviceIdType.MESH
MODEL = 6400
HEAD = 128
HEADS = 5
COLS = (HEADS + 1) * HEAD
TOK = 128
SHARD = 1024
N_CTX = 16
N_EXP = 8
SLOTS = 32
FCH = 5
FW = MODEL // FCH
PCH = 4
PR = TOK // PCH
PH = PR // 2
PM = N_EXP * PR
WROWS = 400
WA = 208
WB = WROWS - WA
EPS = 1e-06
VMEM_LIMIT = 56 * 1024 * 1024


def rms_rows(values, gain):
    mean_square = jnp.mean(values * values, axis=-1, keepdims=True)
    return values * lax.rsqrt(mean_square + EPS) * gain


def exchange_kernel(
    res_hbm, sh_hbm, ex_hbm, eid_ref, gate_ref, gain_ref, wq_hbm, wkv_hbm, qg_ref, kg_ref,
    hid_hbm, q_hbm, kv_hbm,
    slots, res, sh, summed, hid, xall, wall, qbuf, kvbuf,
    loc_sem, a_send, a_recv, a_own, w_send, w_recv1, w_recv2, x_send, x_recv, f_send, f_recv, s_send, s_recv,
    h_send, h_recv, hs_send, hs_recv, out_sem,
):
    c = lax.axis_index("ctx")
    e = lax.axis_index("exp")
    x, z = c // 4, c % 4
    y, k = e // 2, e % 2

    def along_x(d):
        return (((x + d) % 4) * 4 + z, e)

    def along_z(d):
        return (x * 4 + (z + d) % 4, e)

    def along_y(d):
        return (c, ((y + d) % 4) * 2 + k)

    def along_ctx(d):
        return ((c + d + N_CTX) % N_CTX, e)

    sibling = (c, y * 2 + (1 - k))

    def remote(src, dst, send, recv, to):
        pltpu.make_async_remote_copy(
            src_ref=src, dst_ref=dst, send_sem=send, recv_sem=recv, device_id=to, device_id_type=MESH
        ).start()

    def done(ref, sem):
        pltpu.make_async_copy(ref, ref, sem).wait()

    w_own = wall.at[pl.ds(pl.multiple_of(c * WROWS, 16), WROWS), :]
    load_q = pltpu.make_async_copy(wq_hbm, w_own.at[:, : HEADS * HEAD], loc_sem.at[0])
    load_q.start()
    kv_column = pl.multiple_of(e * HEAD, HEAD)
    load_kv = pltpu.make_async_copy(
        wkv_hbm.at[:, pl.ds(kv_column, HEAD)], w_own.at[:, HEADS * HEAD :], loc_sem.at[1]
    )
    load_kv.start()
    load_res = pltpu.make_async_copy(res_hbm, res, loc_sem.at[2])
    load_res.start()
    load_sh = pltpu.make_async_copy(sh_hbm, sh, loc_sem.at[3])
    load_sh.start()
    mine = pl.ds(pl.multiple_of(e * SLOTS, SLOTS), SLOTS)
    for f in range(FCH):
        pltpu.make_async_copy(
            ex_hbm.at[e, :, pl.ds(f * FW, FW)], slots.at[f, mine, :], a_own.at[f]
        ).start()

    barrier = pltpu.get_barrier_semaphore()
    for d in range(1, N_EXP):
        pl.semaphore_signal(barrier, inc=1, device_id=(c, (e + d) % N_EXP), device_id_type=MESH)
    for d in range(1, 4):
        pl.semaphore_signal(barrier, inc=1, device_id=along_x(d), device_id_type=MESH)
        pl.semaphore_signal(barrier, inc=1, device_id=along_z(d), device_id_type=MESH)
    for d in (-2, -1, 1, 2):
        pl.semaphore_signal(barrier, inc=1, device_id=along_ctx(d), device_id_type=MESH)
    pl.semaphore_wait(barrier, (N_EXP - 1) + 6 + 4)

    @pl.loop(0, FCH)
    def _(f):
        columns = pl.ds(pl.multiple_of(f * FW, 128), FW)
        for d in range(1, N_EXP):
            to = (e + d) % N_EXP
            remote(ex_hbm.at[to, :, columns], slots.at[f, mine, :], a_send, a_recv.at[f], (c, to))

    def half_a(index):
        return wall.at[pl.ds(pl.multiple_of(index * WROWS, 16), WA), :]

    def half_b(index):
        return wall.at[pl.ds(pl.multiple_of(index * WROWS + WA, 16), WB), :]

    load_q.wait()
    load_kv.wait()
    for d in (1, 3, 2):
        remote(half_a(c), half_a(c), w_send.at[0], w_recv1.at[0, d], along_x(d))
        remote(half_b(c), half_b(c), w_send.at[1], w_recv1.at[1, d], along_z(d))
    for d in (1, 3, 2):
        remote(half_a(c), half_a(c), w_send.at[0], w_recv2.at[0], along_z(d))
        remote(half_b(c), half_b(c), w_send.at[1], w_recv2.at[1], along_x(d))

    experts = 2 * N_EXP
    chosen = eid_ref[...]
    named = jnp.where(chosen == lax.broadcasted_iota(jnp.int32, (experts, TOK), 0), 1.0, 0.0)
    earlier = lax.broadcasted_iota(jnp.int32, (TOK, TOK), 0) < lax.broadcasted_iota(
        jnp.int32, (TOK, TOK), 1
    )
    before = jnp.dot(
        named.astype(jnp.bfloat16),
        jnp.where(earlier, 1.0, 0.0).astype(jnp.bfloat16),
        preferred_element_type=jnp.float32,
    )
    slot = jnp.sum(named * before, axis=0, keepdims=True)
    row = chosen.astype(jnp.float32) * float(SLOTS // 2) + slot
    place = lax.broadcasted_iota(jnp.int32, (N_EXP * SLOTS, TOK), 0).astype(jnp.float32)
    pick = jnp.where(place == row, 1.0, 0.0).T.astype(jnp.bfloat16)
    gate = jnp.broadcast_to(gate_ref[...], (TOK, TOK)).T[:, :1]

    for d in (1, 3, 2):
        done(half_a(0), w_recv1.at[0, d])
        got = ((x - d + 4) % 4) * 4 + z
        for d2 in (1, 3, 2):
            remote(half_a(got), half_a(got), w_send.at[0], w_recv2.at[0], along_z(d2))
        done(half_b(0), w_recv1.at[1, d])
        got = x * 4 + (z - d + 4) % 4
        for d2 in (1, 3, 2):
            remote(half_b(got), half_b(got), w_send.at[1], w_recv2.at[1], along_x(d2))

    load_res.wait()
    load_sh.wait()
    squares = jnp.zeros((TOK, 1), jnp.float32)
    for f in range(FCH):
        done(slots.at[f, pl.ds(0, SLOTS), :], a_own.at[f])
        done(slots.at[f, pl.ds(0, SLOTS * (N_EXP - 1)), :], a_recv.at[f])
        columns = pl.ds(f * FW, FW)
        routed = jnp.dot(pick, slots[f], preferred_element_type=jnp.float32)
        total = (
            res[:, columns].astype(jnp.float32) + sh[:, columns].astype(jnp.float32) + gate * routed
        )
        hid[:, columns] = total.astype(jnp.bfloat16)
        summed[:, columns] = total
        squares = squares + jnp.sum(total * total, axis=1, keepdims=True)
    scale = lax.rsqrt(squares * (1.0 / MODEL) + EPS)
    here = pl.ds(pl.multiple_of(e * PR, PR), PR)
    gain = gain_ref[...][None, :]
    for p in range(PCH):
        rows = slice(p * PR, (p + 1) * PR)
        xall[p, here, :] = (summed[rows, :] * scale[rows] * gain).astype(jnp.bfloat16)
        block = xall.at[p, here, :]
        remote(block, block, x_send, x_recv.at[p, 0], along_y(1))
        remote(block, block, x_send, x_recv.at[p, 1], along_y(3))
        remote(block, block, s_send, s_recv.at[p], sibling)
    store_hid = pltpu.make_async_copy(hid, hid_hbm, out_sem.at[0])
    store_hid.start()

    def rows_of(p, d, start, count):
        source = ((y + d + 4) % 4) * 2 + k
        return xall.at[p, pl.ds(pl.multiple_of(source * PR + start, 16), count), :]

    @pl.loop(0, PCH)
    def _(p):
        for side, d in ((0, -1), (1, 1)):
            block = rows_of(p, d, 0, PR)
            done(block, x_recv.at[p, side])
            part = rows_of(p, d, side * PH, PH)
            remote(part, part, f_send, f_recv.at[p, side], along_y(-d))
            remote(block, block, s_send, s_recv.at[p], sibling)

    done(wall.at[pl.ds(0, 12 * WA), :], w_recv2.at[0])
    done(wall.at[pl.ds(0, 12 * WB), :], w_recv2.at[1])

    def pass_halo(p):
        for dist in (1, 2):
            part = kv_hbm.at[2 - dist, k, :, p]
            done(part, h_recv.at[p, dist])
            remote(part, part, hs_send, hs_recv, sibling)

    @pl.loop(0, PCH)
    def _(p):
        for side in range(2):
            part = rows_of(p, 2, side * PH, PH)
            done(part, f_recv.at[p, side])
            remote(part, part, s_send, s_recv.at[p], sibling)
        done(xall.at[p, pl.ds(0, 4 * PR), :], s_recv.at[p])

        last = jnp.dot(
            xall[p], wall[:, (HEADS - 1) * HEAD :], preferred_element_type=jnp.float32
        )
        raw = last[:, HEAD:]
        part = jnp.where(k == 0, rms_rows(raw, kg_ref[...]), raw).astype(jnp.bfloat16)
        kvbuf[p] = part.reshape(N_EXP, PR, HEAD)
        for dist in (2, 1):
            remote(
                kvbuf.at[p], kv_hbm.at[2 - dist, k, :, p], h_send, h_recv.at[p, dist], along_ctx(dist)
            )
        remote(kvbuf.at[p], kv_hbm.at[2, k, :, p], hs_send, hs_recv, sibling)
        pltpu.make_async_copy(kvbuf.at[p], kv_hbm.at[2, k, :, p], out_sem.at[1]).start()
        head = rms_rows(last[:, :HEAD], qg_ref[...]).astype(jnp.bfloat16)
        qbuf[p, :, :, (HEADS - 1) * HEAD :] = head.reshape(N_EXP, PR, HEAD)
        for pair in range((HEADS - 1) // 2):
            low = pair * 2 * HEAD
            raw = jnp.dot(
                xall[p], wall[:, low : low + 2 * HEAD], preferred_element_type=jnp.float32
            )
            for i in range(2):
                head = rms_rows(raw[:, i * HEAD : (i + 1) * HEAD], qg_ref[...]).astype(jnp.bfloat16)
                qbuf[p, :, :, low + i * HEAD : low + (i + 1) * HEAD] = head.reshape(N_EXP, PR, HEAD)
        pltpu.make_async_copy(qbuf.at[p], q_hbm.at[:, p], out_sem.at[2]).start()

        @pl.when(p > 0)
        def _():
            pass_halo(p - 1)

    pass_halo(PCH - 1)

    done(ex_hbm.at[pl.ds(0, N_EXP - 1)], a_send)
    done(wall.at[pl.ds(0, 15 * WA), :], w_send.at[0])
    done(wall.at[pl.ds(0, 15 * WB), :], w_send.at[1])
    done(xall.at[:, pl.ds(0, 2 * PR), :], x_send)
    done(xall.at[:, pl.ds(0, PR), :], f_send)
    done(xall.at[:, pl.ds(0, 4 * PR), :], s_send)
    done(kv_hbm.at[pl.ds(0, 2), 0], h_send)
    done(kv_hbm.at[:, 0], hs_send)
    done(kv_hbm.at[:, 0], hs_recv)
    store_hid.wait()
    done(kv_hbm.at[0, 0], out_sem.at[1])
    done(q_hbm, out_sem.at[2])


def exchange(residual, shared_out, expert_rows, expert_id, gate, gain, w_query, w_kv, q_gain, k_gain):
    any_space = pl.BlockSpec(memory_space=pl.ANY)
    vmem = pl.BlockSpec(memory_space=pltpu.VMEM)
    dma = pltpu.SemaphoreType.DMA
    bf16, f32 = jnp.bfloat16, jnp.float32
    return pl.pallas_call(
        exchange_kernel,
        out_shape=(
            jax.ShapeDtypeStruct((TOK, MODEL), bf16),
            jax.ShapeDtypeStruct((N_EXP, PCH, PR, HEADS * HEAD), bf16),
            jax.ShapeDtypeStruct((3, 2, N_EXP, PCH, PR, HEAD), bf16),
        ),
        in_specs=[any_space] * 3 + [vmem] * 3 + [any_space] * 2 + [vmem] * 2,
        out_specs=(any_space, any_space, any_space),
        scratch_shapes=[
            pltpu.VMEM((FCH, N_EXP * SLOTS, FW), bf16),
            pltpu.VMEM((TOK, MODEL), bf16),
            pltpu.VMEM((TOK, MODEL), bf16),
            pltpu.VMEM((TOK, MODEL), f32),
            pltpu.VMEM((TOK, MODEL), bf16),
            pltpu.VMEM((PCH, PM, MODEL), bf16),
            pltpu.VMEM((MODEL, COLS), bf16),
            pltpu.VMEM((PCH, N_EXP, PR, HEADS * HEAD), bf16),
            pltpu.VMEM((PCH, N_EXP, PR, HEAD), bf16),
            dma((4,)),
            dma,
            dma((FCH,)),
            dma((FCH,)),
            dma((2,)),
            dma((2, 4)),
            dma((2,)),
            dma,
            dma((PCH, 2)),
            dma,
            dma((PCH, 2)),
            dma,
            dma((PCH,)),
            dma,
            dma((PCH, 3)),
            dma,
            dma,
            dma((3,)),
        ],
        compiler_params=pltpu.CompilerParams(
            collective_id=0, has_side_effects=True, vmem_limit_bytes=VMEM_LIMIT
        ),
        cost_estimate=pl.CostEstimate(
            flops=2 * SHARD * MODEL * COLS, bytes_accessed=16 * 1024 * 1024, transcendentals=0
        ),
        name="exchange",
    )(residual, shared_out, expert_rows, expert_id, gate, gain, w_query, w_kv, q_gain, k_gain)


BQ = 512
BK = 512
NEG = -1e30
FACTOR = HEAD ** (-0.5) * math.log2(math.e)


def attention_kernel(
    doc_ref, q_ref, kv_ref, hid_hbm, out_ref, hid_out_hbm, values_t, queries_t, s_ref, m_ref, l_ref,
    acc_ref, hid, sem,
):
    c = lax.axis_index("ctx")
    qb = pl.program_id(0)
    steps = SHARD // BQ
    per = SHARD // BK
    load_hid = pltpu.make_async_copy(hid_hbm, hid, sem.at[0])
    store_hid = pltpu.make_async_copy(hid, hid_out_hbm, sem.at[1])

    @pl.when(qb == 0)
    def _():
        load_hid.start()
        for part in range(3):
            values_t[:, part * SHARD : (part + 1) * SHARD] = kv_ref[part, 1].T

    queries_t[...] = q_ref[...].T

    window = (c - 2) * SHARD
    q_low = 2 * SHARD + qb * BQ
    position = q_low + lax.broadcasted_iota(jnp.int32, (1, BQ), 1)

    def starts(i, carried):
        end, first, least, most = carried
        end = end + doc_ref[i]
        first = jnp.where(end <= position, end, first)
        least = jnp.where(end <= q_low, end, least)
        most = jnp.where(end <= q_low + BQ - 1, end, most)
        return end, first, least, most

    _, first, least, most = lax.fori_loop(
        0, doc_ref.shape[0], starts,
        (0 - window, jnp.zeros((1, BQ), jnp.int32) - window, 0 - window, 0 - window),
    )
    low, high = least // BK, (q_low + BQ) // BK
    m_ref[...] = jnp.full(m_ref.shape, NEG, jnp.float32)

    def score(kb, masked):
        k_low = pl.multiple_of(kb * BK, BK)
        keys = kv_ref.at[kb // per, 0][pl.ds(pl.multiple_of((kb % per) * BK, BK), BK), :]
        if masked:
            k_position = k_low + lax.broadcasted_iota(jnp.int32, (BK, BQ), 0)
            allowed = (k_position >= first) & (k_position <= position)
        for h in range(HEADS):
            scores = jnp.dot(
                keys, queries_t[h * HEAD : (h + 1) * HEAD, :], preferred_element_type=jnp.float32
            )
            if masked:
                scores = jnp.where(allowed, scores, NEG)
            s_ref[h, pl.ds(k_low, BK), :] = scores
            m_ref[h] = jnp.maximum(m_ref[h], jnp.max(scores.reshape(BK // 8, 8, BQ), axis=0))

    @pl.loop(low, high)
    def _(kb):
        edge = (kb * BK < most) | (kb * BK + BK > q_low + 1)
        pl.when(edge)(lambda: score(kb, True))
        pl.when(jnp.logical_not(edge))(lambda: score(kb, False))

    for h in range(HEADS):
        largest = jnp.max(m_ref[h], axis=0, keepdims=True) * FACTOR
        m_ref[h] = jnp.broadcast_to(largest, (8, BQ))
    l_ref[...] = jnp.zeros(l_ref.shape, jnp.float32)
    acc_ref[...] = jnp.zeros(acc_ref.shape, jnp.float32)

    @pl.loop(low, high)
    def _(kb):
        k_low = pl.multiple_of(kb * BK, BK)
        values = values_t[:, pl.ds(k_low, BK)]
        for h in range(HEADS):
            scores = s_ref[h, pl.ds(k_low, BK), :].reshape(BK // 8, 8, BQ)
            weights = jnp.exp2(scores * FACTOR - m_ref[h][None])
            l_ref[h] += jnp.sum(weights, axis=0)
            acc_ref[h] += jnp.dot(
                values, weights.reshape(BK, BQ).astype(jnp.bfloat16),
                preferred_element_type=jnp.float32,
            )

    for h in range(HEADS):
        total = jnp.sum(l_ref[h], axis=0, keepdims=True)
        out_ref[:, h * HEAD : (h + 1) * HEAD] = (acc_ref[h] / total).T.astype(jnp.bfloat16)

    @pl.when(qb == 0)
    def _():
        load_hid.wait()
        store_hid.start()

    @pl.when(qb == steps - 1)
    def _():
        store_hid.wait()


def attention(doc_lengths, queries, kv, hidden):
    any_space = pl.BlockSpec(memory_space=pl.ANY)
    vmem = pltpu.VMEM
    f32, bf16 = jnp.float32, jnp.bfloat16
    return pl.pallas_call(
        attention_kernel,
        grid=(SHARD // BQ,),
        out_shape=(
            jax.ShapeDtypeStruct((SHARD, HEADS * HEAD), bf16),
            jax.ShapeDtypeStruct((TOK, MODEL), bf16),
        ),
        in_specs=[
            pl.BlockSpec(memory_space=pltpu.SMEM),
            pl.BlockSpec((BQ, HEADS * HEAD), lambda i: (i, 0)),
            pl.BlockSpec((3, 2, SHARD, HEAD), lambda i: (0, 0, 0, 0)),
            any_space,
        ],
        out_specs=(pl.BlockSpec((BQ, HEADS * HEAD), lambda i: (i, 0)), any_space),
        scratch_shapes=[
            vmem((HEAD, 3 * SHARD), bf16),
            vmem((HEADS * HEAD, BQ), bf16),
            vmem((HEADS, 3 * SHARD, BQ), f32),
            vmem((HEADS, 8, BQ), f32),
            vmem((HEADS, 8, BQ), f32),
            vmem((HEADS, HEAD, BQ), f32),
            vmem((TOK, MODEL), bf16),
            pltpu.SemaphoreType.DMA((2,)),
        ],
        compiler_params=pltpu.CompilerParams(vmem_limit_bytes=VMEM_LIMIT),
        name="attention",
    )(doc_lengths, queries, kv, hidden)


def per_device(
    residual, shared_out, expert_out, expert_id, gate_value, doc_lengths, norm_gain, w_query,
    key_value_weight, query_gain, key_gain,
):
    hidden, queries, kv = exchange(
        residual,
        shared_out,
        expert_out.reshape(N_EXP, SLOTS, MODEL),
        expert_id.reshape(1, TOK),
        gate_value.reshape(1, TOK),
        norm_gain,
        w_query,
        key_value_weight,
        query_gain.reshape(1, HEAD),
        key_gain.reshape(1, HEAD),
    )
    attended, hidden_out = attention(
        doc_lengths, queries.reshape(SHARD, HEADS * HEAD), kv.reshape(3, 2, SHARD, HEAD), hidden
    )
    return (hidden_out, attended)


def solution(mesh):
    placed = (
        P(("ctx", "exp"), None),
        P(("ctx", "exp"), None),
        P("ctx", "exp", None, None, None, None),
        P(("ctx", "exp"), None),
        P(("ctx", "exp"), None),
        P(),
        P(),
        P("ctx", "exp"),
        P("ctx", None),
        P(),
        P(),
    )
    return jax.shard_map(
        per_device,
        mesh=mesh,
        in_specs=placed,
        out_specs=(P(("ctx", "exp"), None), P("ctx", "exp")),
        check_vma=False,
    )
```

```python
import functools
import math

import jax
import jax.numpy as jnp
from jax import lax
from jax.experimental import pallas as pl
from jax.experimental.pallas import tpu as pltpu
from jax.sharding import PartitionSpec as P

MESH = pl.DeviceIdType.MESH
MODEL = 6400
HEAD = 128
HEADS = 5
COLS = (HEADS + 1) * HEAD
TOK = 128
SHARD = 1024
N_CTX = 16
N_EXP = 8
SLOTS = 32
FCH = 5
FW = MODEL // FCH
PCH = 8
PR = TOK // PCH
AHEAD = 3
PM = N_EXP * PR
WROWS = 400
WA = 208
WB = WROWS - WA
EPS = 1e-06
VMEM_LIMIT = 56 * 1024 * 1024


def rms_rows(values, gain):
    mean_square = jnp.mean(values * values, axis=-1, keepdims=True)
    return values * lax.rsqrt(mean_square + EPS) * gain


def exchange_kernel(
    res_hbm, sh_hbm, ex_hbm, eid_ref, gate_ref, gain_ref, wq_hbm, wkv_hbm, qg_ref, kg_ref,
    hid_hbm, q_hbm, kv_hbm,
    slots, res, sh, summed, hid, xall, wall, qbuf, kvbuf,
    loc_sem, a_send, a_recv, a_own, w_send, w_recv1, w_recv2, x_send, x_recv, f_send, f_recv, s_send, s_recv,
    h_send, h_recv, hs_send, hs_recv, out_sem,
):
    c = lax.axis_index("ctx")
    e = lax.axis_index("exp")
    x, z = c // 4, c % 4
    y, k = e // 2, e % 2

    def along_x(d):
        return (((x + d) % 4) * 4 + z, e)

    def along_z(d):
        return (x * 4 + (z + d) % 4, e)

    def along_y(d):
        return (c, ((y + d) % 4) * 2 + k)

    def along_ctx(d):
        return ((c + d + N_CTX) % N_CTX, e)

    sibling = (c, y * 2 + (1 - k))

    def remote(src, dst, send, recv, to):
        pltpu.make_async_remote_copy(
            src_ref=src, dst_ref=dst, send_sem=send, recv_sem=recv, device_id=to, device_id_type=MESH
        ).start()

    def done(ref, sem):
        pltpu.make_async_copy(ref, ref, sem).wait()

    w_own = wall.at[pl.ds(pl.multiple_of(c * WROWS, 16), WROWS), :]
    load_q = pltpu.make_async_copy(wq_hbm, w_own.at[:, : HEADS * HEAD], loc_sem.at[0])
    load_q.start()
    kv_column = pl.multiple_of(e * HEAD, HEAD)
    load_kv = pltpu.make_async_copy(
        wkv_hbm.at[:, pl.ds(kv_column, HEAD)], w_own.at[:, HEADS * HEAD :], loc_sem.at[1]
    )
    load_kv.start()
    load_res = pltpu.make_async_copy(res_hbm, res, loc_sem.at[2])
    load_res.start()
    load_sh = pltpu.make_async_copy(sh_hbm, sh, loc_sem.at[3])
    load_sh.start()
    mine = pl.ds(pl.multiple_of(e * SLOTS, SLOTS), SLOTS)
    for f in range(FCH):
        pltpu.make_async_copy(
            ex_hbm.at[e, :, pl.ds(f * FW, FW)], slots.at[f, mine, :], a_own.at[f]
        ).start()

    barrier = pltpu.get_barrier_semaphore()
    for d in range(1, N_EXP):
        pl.semaphore_signal(barrier, inc=1, device_id=(c, (e + d) % N_EXP), device_id_type=MESH)
    for d in range(1, 4):
        pl.semaphore_signal(barrier, inc=1, device_id=along_x(d), device_id_type=MESH)
        pl.semaphore_signal(barrier, inc=1, device_id=along_z(d), device_id_type=MESH)
    for d in (-2, -1, 1, 2):
        pl.semaphore_signal(barrier, inc=1, device_id=along_ctx(d), device_id_type=MESH)
    pl.semaphore_wait(barrier, (N_EXP - 1) + 6 + 4)

    @pl.loop(0, FCH)
    def _(f):
        columns = pl.ds(pl.multiple_of(f * FW, 128), FW)
        for d in range(1, N_EXP):
            to = (e + d) % N_EXP
            remote(ex_hbm.at[to, :, columns], slots.at[f, mine, :], a_send, a_recv.at[f], (c, to))

    def half_a(index):
        return wall.at[pl.ds(pl.multiple_of(index * WROWS, 16), WA), :]

    def half_b(index):
        return wall.at[pl.ds(pl.multiple_of(index * WROWS + WA, 16), WB), :]

    load_q.wait()
    load_kv.wait()
    for d in (1, 3, 2):
        remote(half_a(c), half_a(c), w_send.at[0], w_recv1.at[0, d], along_x(d))
        remote(half_b(c), half_b(c), w_send.at[1], w_recv1.at[1, d], along_z(d))
    for d in (1, 3, 2):
        remote(half_a(c), half_a(c), w_send.at[0], w_recv2.at[0], along_z(d))
        remote(half_b(c), half_b(c), w_send.at[1], w_recv2.at[1], along_x(d))

    experts = 2 * N_EXP
    chosen = eid_ref[...]
    named = jnp.where(chosen == lax.broadcasted_iota(jnp.int32, (experts, TOK), 0), 1.0, 0.0)
    earlier = lax.broadcasted_iota(jnp.int32, (TOK, TOK), 0) < lax.broadcasted_iota(
        jnp.int32, (TOK, TOK), 1
    )
    before = jnp.dot(
        named.astype(jnp.bfloat16),
        jnp.where(earlier, 1.0, 0.0).astype(jnp.bfloat16),
        preferred_element_type=jnp.float32,
    )
    slot = jnp.sum(named * before, axis=0, keepdims=True)
    row = chosen.astype(jnp.float32) * float(SLOTS // 2) + slot
    place = lax.broadcasted_iota(jnp.int32, (N_EXP * SLOTS, TOK), 0).astype(jnp.float32)
    pick = jnp.where(place == row, 1.0, 0.0).T.astype(jnp.bfloat16)
    gate = jnp.broadcast_to(gate_ref[...], (TOK, TOK)).T[:, :1]

    for d in (1, 3, 2):
        done(half_a(0), w_recv1.at[0, d])
        got = ((x - d + 4) % 4) * 4 + z
        for d2 in (1, 3, 2):
            remote(half_a(got), half_a(got), w_send.at[0], w_recv2.at[0], along_z(d2))
        done(half_b(0), w_recv1.at[1, d])
        got = x * 4 + (z - d + 4) % 4
        for d2 in (1, 3, 2):
            remote(half_b(got), half_b(got), w_send.at[1], w_recv2.at[1], along_x(d2))

    load_res.wait()
    load_sh.wait()
    squares = jnp.zeros((TOK, 1), jnp.float32)
    for f in range(FCH):
        done(slots.at[f, pl.ds(0, SLOTS), :], a_own.at[f])
        done(slots.at[f, pl.ds(0, SLOTS * (N_EXP - 1)), :], a_recv.at[f])
        columns = pl.ds(f * FW, FW)
        routed = jnp.dot(pick, slots[f], preferred_element_type=jnp.float32)
        total = (
            res[:, columns].astype(jnp.float32) + sh[:, columns].astype(jnp.float32) + gate * routed
        )
        hid[:, columns] = total.astype(jnp.bfloat16)
        summed[:, columns] = total
        squares = squares + jnp.sum(total * total, axis=1, keepdims=True)
    scale = lax.rsqrt(squares * (1.0 / MODEL) + EPS)
    here = pl.ds(pl.multiple_of(e * PR, PR), PR)
    gain = gain_ref[...][None, :]
    def rows_of(p, d):
        source = ((y + d + 4) % 4) * 2 + k
        return xall.at[p, pl.ds(pl.multiple_of(source * PR, PR), PR), :]

    def send_chunk(p):
        block = rows_of(p, 0)
        remote(block, block, x_send, x_recv.at[p, 0], along_y(1))
        remote(block, block, x_send, x_recv.at[p, 1], along_y(3))
        remote(block, block, s_send, s_recv.at[p], sibling)

    for p in range(PCH):
        rows = slice(p * PR, (p + 1) * PR)
        xall[p, here, :] = (summed[rows, :] * scale[rows] * gain).astype(jnp.bfloat16)
        if p < AHEAD:
            send_chunk(p)
    store_hid = pltpu.make_async_copy(hid, hid_hbm, out_sem.at[0])
    store_hid.start()

    def pass_on(p):
        up = 1 - 2 * (p % 2)
        done(rows_of(p, -1), x_recv.at[p, 0])
        done(rows_of(p, 1), x_recv.at[p, 1])
        part = rows_of(p, -up)
        remote(part, part, f_send, f_recv.at[p], along_y(up))
        for d in (-1, 1):
            block = rows_of(p, d)
            remote(block, block, s_send, s_recv.at[p], sibling)

        @pl.when(p < PCH - AHEAD)
        def _():
            send_chunk(p + AHEAD)

    @pl.loop(0, PCH // 2)
    def _(p):
        pass_on(p)

    done(wall.at[pl.ds(0, 12 * WA), :], w_recv2.at[0])
    done(wall.at[pl.ds(0, 12 * WB), :], w_recv2.at[1])

    def pass_halo(p):
        for dist in (1, 2):
            part = kv_hbm.at[k, 2 - dist, :, p]
            done(part, h_recv.at[p, dist])
            remote(part, part, hs_send, hs_recv, sibling)

    @pl.loop(0, PCH)
    def _(p):
        @pl.when((p >= PCH // 2 - 2) & (p < PCH - 2))
        def _():
            pass_on(p + 2)

        part = rows_of(p, 2)
        done(part, f_recv.at[p])
        remote(part, part, s_send, s_recv.at[p], sibling)
        done(xall.at[p, pl.ds(0, 4 * PR), :], s_recv.at[p])

        last = jnp.dot(
            xall[p], wall[:, (HEADS - 1) * HEAD :], preferred_element_type=jnp.float32
        )
        raw = last[:, HEAD:]
        part = jnp.where(k == 0, rms_rows(raw, kg_ref[...]), raw).astype(jnp.bfloat16)
        kvbuf[p] = part.reshape(N_EXP, PR, HEAD)
        for dist in (2, 1):
            remote(
                kvbuf.at[p], kv_hbm.at[k, 2 - dist, :, p], h_send, h_recv.at[p, dist], along_ctx(dist)
            )
        remote(kvbuf.at[p], kv_hbm.at[k, 2, :, p], hs_send, hs_recv, sibling)
        pltpu.make_async_copy(kvbuf.at[p], kv_hbm.at[k, 2, :, p], out_sem.at[1]).start()
        head = rms_rows(last[:, :HEAD], qg_ref[...]).astype(jnp.bfloat16)
        qbuf[p, :, :, (HEADS - 1) * HEAD :] = head.reshape(N_EXP, PR, HEAD)
        for pair in range((HEADS - 1) // 2):
            low = pair * 2 * HEAD
            raw = jnp.dot(
                xall[p], wall[:, low : low + 2 * HEAD], preferred_element_type=jnp.float32
            )
            for i in range(2):
                head = rms_rows(raw[:, i * HEAD : (i + 1) * HEAD], qg_ref[...]).astype(jnp.bfloat16)
                qbuf[p, :, :, low + i * HEAD : low + (i + 1) * HEAD] = head.reshape(N_EXP, PR, HEAD)
        pltpu.make_async_copy(qbuf.at[p], q_hbm.at[:, p], out_sem.at[2]).start()

        @pl.when(p > 0)
        def _():
            pass_halo(p - 1)

    pass_halo(PCH - 1)

    done(ex_hbm.at[pl.ds(0, N_EXP - 1)], a_send)
    done(wall.at[pl.ds(0, 15 * WA), :], w_send.at[0])
    done(wall.at[pl.ds(0, 15 * WB), :], w_send.at[1])
    done(xall.at[:, pl.ds(0, 2 * PR), :], x_send)
    done(xall.at[:, pl.ds(0, PR), :], f_send)
    done(xall.at[:, pl.ds(0, 4 * PR), :], s_send)
    done(kv_hbm.at[0, pl.ds(0, 2)], h_send)
    done(kv_hbm.at[0], hs_send)
    done(kv_hbm.at[0], hs_recv)
    store_hid.wait()
    done(kv_hbm.at[0, 0], out_sem.at[1])
    done(q_hbm, out_sem.at[2])


def exchange(residual, shared_out, expert_rows, expert_id, gate, gain, w_query, w_kv, q_gain, k_gain):
    any_space = pl.BlockSpec(memory_space=pl.ANY)
    vmem = pl.BlockSpec(memory_space=pltpu.VMEM)
    dma = pltpu.SemaphoreType.DMA
    bf16, f32 = jnp.bfloat16, jnp.float32
    return pl.pallas_call(
        exchange_kernel,
        out_shape=(
            jax.ShapeDtypeStruct((TOK, MODEL), bf16),
            jax.ShapeDtypeStruct((N_EXP, PCH, PR, HEADS * HEAD), bf16),
            jax.ShapeDtypeStruct((2, 3, N_EXP, PCH, PR, HEAD), bf16),
        ),
        in_specs=[any_space] * 3 + [vmem] * 3 + [any_space] * 2 + [vmem] * 2,
        out_specs=(any_space, any_space, any_space),
        scratch_shapes=[
            pltpu.VMEM((FCH, N_EXP * SLOTS, FW), bf16),
            pltpu.VMEM((TOK, MODEL), bf16),
            pltpu.VMEM((TOK, MODEL), bf16),
            pltpu.VMEM((TOK, MODEL), f32),
            pltpu.VMEM((TOK, MODEL), bf16),
            pltpu.VMEM((PCH, PM, MODEL), bf16),
            pltpu.VMEM((MODEL, COLS), bf16),
            pltpu.VMEM((PCH, N_EXP, PR, HEADS * HEAD), bf16),
            pltpu.VMEM((PCH, N_EXP, PR, HEAD), bf16),
            dma((4,)),
            dma,
            dma((FCH,)),
            dma((FCH,)),
            dma((2,)),
            dma((2, 4)),
            dma((2,)),
            dma,
            dma((PCH, 2)),
            dma,
            dma((PCH,)),
            dma,
            dma((PCH,)),
            dma,
            dma((PCH, 3)),
            dma,
            dma,
            dma((3,)),
        ],
        compiler_params=pltpu.CompilerParams(
            collective_id=0, has_side_effects=True, vmem_limit_bytes=VMEM_LIMIT
        ),
        cost_estimate=pl.CostEstimate(
            flops=2 * SHARD * MODEL * COLS, bytes_accessed=16 * 1024 * 1024, transcendentals=0
        ),
        name="exchange",
    )(residual, shared_out, expert_rows, expert_id, gate, gain, w_query, w_kv, q_gain, k_gain)


BQ = 512
BK = 512
NEG = -1e30
FACTOR = HEAD ** (-0.5) * math.log2(math.e)


def attention_kernel(
    doc_ref, q_ref, kv_ref, hid_hbm, out_ref, hid_out_hbm, values_t, queries_t, s_ref, m_ref, l_ref,
    acc_ref, hid, sem,
):
    c = lax.axis_index("ctx")
    qb = pl.program_id(0)
    steps = SHARD // BQ
    load_hid = pltpu.make_async_copy(hid_hbm, hid, sem.at[0])
    store_hid = pltpu.make_async_copy(hid, hid_out_hbm, sem.at[1])

    @pl.when(qb == 0)
    def _():
        load_hid.start()
        values_t[...] = kv_ref[1].T

    queries_t[...] = q_ref[...].T

    window = (c - 2) * SHARD
    q_low = pl.multiple_of(2 * SHARD + qb * BQ, BQ)
    position = q_low + lax.broadcasted_iota(jnp.int32, (1, BQ), 1)

    def starts(i, carried):
        end, first, least, most = carried
        end = end + doc_ref[i]
        first = jnp.where(end <= position, end, first)
        least = jnp.where(end <= q_low, end, least)
        most = jnp.where(end <= q_low + BQ - 1, end, most)
        return end, first, least, most

    _, first, least, most = lax.fori_loop(
        0, doc_ref.shape[0], starts,
        (0 - window, jnp.zeros((1, BQ), jnp.int32) - window, 0 - window, 0 - window),
    )
    m_ref[...] = jnp.full(m_ref.shape, NEG, jnp.float32)

    def score(k_low, count, skip, masked):
        keys = kv_ref[0, pl.ds(k_low, count), :]
        if masked:
            k_position = k_low + lax.broadcasted_iota(jnp.int32, (count, BQ - skip), 0)
            allowed = (k_position >= first[:, skip:]) & (k_position <= position[:, skip:])
        for h in range(HEADS):
            scores = jnp.dot(
                keys, queries_t[h * HEAD : (h + 1) * HEAD, skip:],
                preferred_element_type=jnp.float32,
            )
            if masked:
                scores = jnp.where(allowed, scores, NEG)
            s_ref[h, pl.ds(k_low, count), skip:] = scores
            m_ref[h, :, skip:] = jnp.maximum(
                m_ref[h, :, skip:], jnp.max(scores.reshape(count // 8, 8, BQ - skip), axis=0)
            )

    def weigh(k_low, count, skip):
        values = values_t[:, pl.ds(k_low, count)]
        for h in range(HEADS):
            scores = s_ref[h, pl.ds(k_low, count), skip:].reshape(count // 8, 8, BQ - skip)
            weights = jnp.exp2(scores * FACTOR - m_ref[h, :, skip:][None])
            l_ref[h, :, skip:] += jnp.sum(weights, axis=0)
            acc_ref[h, :, skip:] += jnp.dot(
                values, weights.reshape(count, BQ - skip).astype(jnp.bfloat16),
                preferred_element_type=jnp.float32,
            )

    half = BK // 2
    low = jnp.minimum(least // half, q_low // half)
    odd = (q_low // half - low) % 2
    whole = (q_low - (low + odd) * half) // BK

    def each_block(act):
        @pl.when(odd == 1)
        def _():
            act(pl.multiple_of(low * half, half), half)

        @pl.loop(0, whole)
        def _(i):
            act(pl.multiple_of((low + odd) * half + i * BK, half), BK)

    def score_block(k_low, count):
        pl.when(k_low < most)(lambda: score(k_low, count, 0, True))
        pl.when(k_low >= most)(lambda: score(k_low, count, 0, False))

    each_block(score_block)
    score(q_low, half, 0, True)
    score(pl.multiple_of(q_low + half, half), half, half, True)

    for h in range(HEADS):
        largest = jnp.max(m_ref[h], axis=0, keepdims=True) * FACTOR
        m_ref[h] = jnp.broadcast_to(largest, (8, BQ))
    l_ref[...] = jnp.zeros(l_ref.shape, jnp.float32)
    acc_ref[...] = jnp.zeros(acc_ref.shape, jnp.float32)

    each_block(lambda k_low, count: weigh(k_low, count, 0))
    weigh(q_low, half, 0)
    weigh(pl.multiple_of(q_low + half, half), half, half)

    for h in range(HEADS):
        total = jnp.sum(l_ref[h], axis=0, keepdims=True)
        out_ref[:, h * HEAD : (h + 1) * HEAD] = (acc_ref[h] / total).T.astype(jnp.bfloat16)

    @pl.when(qb == 0)
    def _():
        load_hid.wait()
        store_hid.start()

    @pl.when(qb == steps - 1)
    def _():
        store_hid.wait()


def attention(doc_lengths, queries, kv, hidden):
    any_space = pl.BlockSpec(memory_space=pl.ANY)
    vmem = pltpu.VMEM
    f32, bf16 = jnp.float32, jnp.bfloat16
    return pl.pallas_call(
        attention_kernel,
        grid=(SHARD // BQ,),
        out_shape=(
            jax.ShapeDtypeStruct((SHARD, HEADS * HEAD), bf16),
            jax.ShapeDtypeStruct((TOK, MODEL), bf16),
        ),
        in_specs=[
            pl.BlockSpec(memory_space=pltpu.SMEM),
            pl.BlockSpec((BQ, HEADS * HEAD), lambda i: (i, 0)),
            pl.BlockSpec((2, 3 * SHARD, HEAD), lambda i: (0, 0, 0)),
            any_space,
        ],
        out_specs=(pl.BlockSpec((BQ, HEADS * HEAD), lambda i: (i, 0)), any_space),
        scratch_shapes=[
            vmem((HEAD, 3 * SHARD), bf16),
            vmem((HEADS * HEAD, BQ), bf16),
            vmem((HEADS, 3 * SHARD, BQ), f32),
            vmem((HEADS, 8, BQ), f32),
            vmem((HEADS, 8, BQ), f32),
            vmem((HEADS, HEAD, BQ), f32),
            vmem((TOK, MODEL), bf16),
            pltpu.SemaphoreType.DMA((2,)),
        ],
        compiler_params=pltpu.CompilerParams(vmem_limit_bytes=VMEM_LIMIT),
        name="attention",
    )(doc_lengths, queries, kv, hidden)


def per_device(
    residual, shared_out, expert_out, expert_id, gate_value, doc_lengths, norm_gain, w_query,
    key_value_weight, query_gain, key_gain,
):
    hidden, queries, kv = exchange(
        residual,
        shared_out,
        expert_out.reshape(N_EXP, SLOTS, MODEL),
        expert_id.reshape(1, TOK),
        gate_value.reshape(1, TOK),
        norm_gain,
        w_query,
        key_value_weight,
        query_gain.reshape(1, HEAD),
        key_gain.reshape(1, HEAD),
    )
    attended, hidden_out = attention(
        doc_lengths, queries.reshape(SHARD, HEADS * HEAD), kv.reshape(2, 3 * SHARD, HEAD), hidden
    )
    return (hidden_out, attended)


def solution(mesh):
    placed = (
        P(("ctx", "exp"), None),
        P(("ctx", "exp"), None),
        P("ctx", "exp", None, None, None, None),
        P(("ctx", "exp"), None),
        P(("ctx", "exp"), None),
        P(),
        P(),
        P("ctx", "exp"),
        P("ctx", None),
        P(),
        P(),
    )
    return jax.shard_map(
        per_device,
        mesh=mesh,
        in_specs=placed,
        out_specs=(P(("ctx", "exp"), None), P("ctx", "exp")),
        check_vma=False,
    )
```

```python
import functools
import math

import jax
import jax.numpy as jnp
from jax import lax
from jax.experimental import pallas as pl
from jax.experimental.pallas import tpu as pltpu
from jax.sharding import PartitionSpec as P

MESH = pl.DeviceIdType.MESH
MODEL = 6400
HEAD = 128
HEADS = 5
COLS = (HEADS + 1) * HEAD
TOK = 128
SHARD = 1024
N_CTX = 16
N_EXP = 8
SLOTS = 32
FCH = 5
FW = MODEL // FCH
PCH = 8
PR = TOK // PCH
AHEAD = 3
PM = N_EXP * PR
WROWS = 400
WA = 208
WB = WROWS - WA
EPS = 1e-06
VMEM_LIMIT = 56 * 1024 * 1024


def rms_rows(values, gain):
    mean_square = jnp.mean(values * values, axis=-1, keepdims=True)
    return values * lax.rsqrt(mean_square + EPS) * gain


def exchange_kernel(
    res_hbm, sh_hbm, ex_hbm, eid_ref, gate_ref, gain_ref, wq_hbm, wkv_hbm, qg_ref, kg_ref,
    hid_hbm, q_hbm, kv_hbm,
    slots, res, sh, summed, hid, xall, wall, qbuf, kvbuf,
    loc_sem, a_send, a_recv, a_own, w_send, w_recv1, w_recv2, x_send, x_recv, f_send, f_recv, s_send, s_recv,
    h_send, h_recv, hs_send, hs_recv, out_sem,
):
    c = lax.axis_index("ctx")
    e = lax.axis_index("exp")
    x, z = c // 4, c % 4
    y, k = e // 2, e % 2

    def along_x(d):
        return (((x + d) % 4) * 4 + z, e)

    def along_z(d):
        return (x * 4 + (z + d) % 4, e)

    def along_y(d):
        return (c, ((y + d) % 4) * 2 + k)

    def along_ctx(d):
        return ((c + d + N_CTX) % N_CTX, e)

    sibling = (c, y * 2 + (1 - k))

    def remote(src, dst, send, recv, to):
        pltpu.make_async_remote_copy(
            src_ref=src, dst_ref=dst, send_sem=send, recv_sem=recv, device_id=to, device_id_type=MESH
        ).start()

    def done(ref, sem):
        pltpu.make_async_copy(ref, ref, sem).wait()

    w_own = wall.at[pl.ds(pl.multiple_of(c * WROWS, 16), WROWS), :]
    load_q = pltpu.make_async_copy(wq_hbm, w_own.at[:, : HEADS * HEAD], loc_sem.at[0])
    load_q.start()
    kv_column = pl.multiple_of(e * HEAD, HEAD)
    load_kv = pltpu.make_async_copy(
        wkv_hbm.at[:, pl.ds(kv_column, HEAD)], w_own.at[:, HEADS * HEAD :], loc_sem.at[1]
    )
    load_kv.start()
    load_res = pltpu.make_async_copy(res_hbm, res, loc_sem.at[2])
    load_res.start()
    load_sh = pltpu.make_async_copy(sh_hbm, sh, loc_sem.at[3])
    load_sh.start()
    mine = pl.ds(pl.multiple_of(e * SLOTS, SLOTS), SLOTS)
    for f in range(FCH):
        pltpu.make_async_copy(
            ex_hbm.at[e, :, pl.ds(f * FW, FW)], slots.at[f, mine, :], a_own.at[f]
        ).start()

    barrier = pltpu.get_barrier_semaphore()
    for d in range(1, N_EXP):
        pl.semaphore_signal(barrier, inc=1, device_id=(c, (e + d) % N_EXP), device_id_type=MESH)
    for d in range(1, 4):
        pl.semaphore_signal(barrier, inc=1, device_id=along_x(d), device_id_type=MESH)
        pl.semaphore_signal(barrier, inc=1, device_id=along_z(d), device_id_type=MESH)
    for d in (-2, -1, 1, 2):
        pl.semaphore_signal(barrier, inc=1, device_id=along_ctx(d), device_id_type=MESH)
    pl.semaphore_wait(barrier, (N_EXP - 1) + 6 + 4)

    @pl.loop(0, FCH)
    def _(f):
        columns = pl.ds(pl.multiple_of(f * FW, 128), FW)
        for d in range(1, N_EXP):
            to = (e + d) % N_EXP
            remote(ex_hbm.at[to, :, columns], slots.at[f, mine, :], a_send, a_recv.at[f], (c, to))

    def half_a(index):
        return wall.at[pl.ds(pl.multiple_of(index * WROWS, 16), WA), :]

    def half_b(index):
        return wall.at[pl.ds(pl.multiple_of(index * WROWS + WA, 16), WB), :]

    load_q.wait()
    load_kv.wait()
    for d in (1, 3, 2):
        remote(half_a(c), half_a(c), w_send.at[0], w_recv1.at[0, d], along_x(d))
        remote(half_b(c), half_b(c), w_send.at[1], w_recv1.at[1, d], along_z(d))
    for d in (1, 3, 2):
        remote(half_a(c), half_a(c), w_send.at[0], w_recv2.at[0], along_z(d))
        remote(half_b(c), half_b(c), w_send.at[1], w_recv2.at[1], along_x(d))

    experts = 2 * N_EXP
    chosen = eid_ref[...]
    named = jnp.where(chosen == lax.broadcasted_iota(jnp.int32, (experts, TOK), 0), 1.0, 0.0)
    earlier = lax.broadcasted_iota(jnp.int32, (TOK, TOK), 0) < lax.broadcasted_iota(
        jnp.int32, (TOK, TOK), 1
    )
    before = jnp.dot(
        named.astype(jnp.bfloat16),
        jnp.where(earlier, 1.0, 0.0).astype(jnp.bfloat16),
        preferred_element_type=jnp.float32,
    )
    slot = jnp.sum(named * before, axis=0, keepdims=True)
    row = chosen.astype(jnp.float32) * float(SLOTS // 2) + slot
    place = lax.broadcasted_iota(jnp.int32, (N_EXP * SLOTS, TOK), 0).astype(jnp.float32)
    pick = jnp.where(place == row, 1.0, 0.0).T.astype(jnp.bfloat16)
    gate = jnp.broadcast_to(gate_ref[...], (TOK, TOK)).T[:, :1]

    for d in (1, 3, 2):
        done(half_a(0), w_recv1.at[0, d])
        got = ((x - d + 4) % 4) * 4 + z
        for d2 in (1, 3, 2):
            remote(half_a(got), half_a(got), w_send.at[0], w_recv2.at[0], along_z(d2))
        done(half_b(0), w_recv1.at[1, d])
        got = x * 4 + (z - d + 4) % 4
        for d2 in (1, 3, 2):
            remote(half_b(got), half_b(got), w_send.at[1], w_recv2.at[1], along_x(d2))

    load_res.wait()
    load_sh.wait()
    squares = jnp.zeros((TOK, 1), jnp.float32)
    for f in range(FCH):
        done(slots.at[f, pl.ds(0, SLOTS), :], a_own.at[f])
        done(slots.at[f, pl.ds(0, SLOTS * (N_EXP - 1)), :], a_recv.at[f])
        columns = pl.ds(f * FW, FW)
        routed = jnp.dot(pick, slots[f], preferred_element_type=jnp.float32)
        total = (
            res[:, columns].astype(jnp.float32) + sh[:, columns].astype(jnp.float32) + gate * routed
        )
        hid[:, columns] = total.astype(jnp.bfloat16)
        summed[:, columns] = total
        squares = squares + jnp.sum(total * total, axis=1, keepdims=True)
    scale = lax.rsqrt(squares * (1.0 / MODEL) + EPS)
    here = pl.ds(pl.multiple_of(e * PR, PR), PR)
    gain = gain_ref[...][None, :]
    def rows_of(p, d):
        source = ((y + d + 4) % 4) * 2 + k
        return xall.at[p, pl.ds(pl.multiple_of(source * PR, PR), PR), :]

    def send_chunk(p):
        block = rows_of(p, 0)
        remote(block, block, x_send, x_recv.at[p, 0], along_y(1))
        remote(block, block, x_send, x_recv.at[p, 1], along_y(3))
        remote(block, block, s_send, s_recv.at[p], sibling)

    for p in range(PCH):
        rows = slice(p * PR, (p + 1) * PR)
        xall[p, here, :] = (summed[rows, :] * scale[rows] * gain).astype(jnp.bfloat16)
        if p < AHEAD:
            send_chunk(p)
    store_hid = pltpu.make_async_copy(hid, hid_hbm, out_sem.at[0])
    store_hid.start()

    def half_of(p, d, side):
        return rows_of(p, d).at[:, pl.ds(side * (MODEL // 2), MODEL // 2)]

    def pass_on(p):
        for side, d in ((0, -1), (1, 1)):
            done(rows_of(p, d), x_recv.at[p, side])
            part = half_of(p, d, side)
            remote(part, part, f_send, f_recv.at[p, side], along_y(-d))
        for d in (-1, 1):
            block = rows_of(p, d)
            remote(block, block, s_send, s_recv.at[p], sibling)

        @pl.when(p < PCH - AHEAD)
        def _():
            send_chunk(p + AHEAD)

    @pl.loop(0, PCH // 2)
    def _(p):
        pass_on(p)

    done(wall.at[pl.ds(0, 12 * WA), :], w_recv2.at[0])
    done(wall.at[pl.ds(0, 12 * WB), :], w_recv2.at[1])

    def pass_halo(p):
        for dist in (1, 2):
            part = kv_hbm.at[k, 2 - dist, :, p]
            done(part, h_recv.at[p, dist])
            remote(part, part, hs_send, hs_recv, sibling)

    @pl.loop(0, PCH)
    def _(p):
        @pl.when((p >= PCH // 2 - 2) & (p < PCH - 2))
        def _():
            pass_on(p + 2)

        for side in range(2):
            done(half_of(p, 2, side), f_recv.at[p, side])
        block = rows_of(p, 2)
        remote(block, block, s_send, s_recv.at[p], sibling)
        done(xall.at[p, pl.ds(0, 4 * PR), :], s_recv.at[p])

        last = jnp.dot(
            xall[p], wall[:, (HEADS - 1) * HEAD :], preferred_element_type=jnp.float32
        )
        raw = last[:, HEAD:]
        part = jnp.where(k == 0, rms_rows(raw, kg_ref[...]), raw).astype(jnp.bfloat16)
        kvbuf[p] = part.reshape(N_EXP, PR, HEAD)
        for dist in (2, 1):
            remote(
                kvbuf.at[p], kv_hbm.at[k, 2 - dist, :, p], h_send, h_recv.at[p, dist], along_ctx(dist)
            )
        remote(kvbuf.at[p], kv_hbm.at[k, 2, :, p], hs_send, hs_recv, sibling)
        pltpu.make_async_copy(kvbuf.at[p], kv_hbm.at[k, 2, :, p], out_sem.at[1]).start()
        head = rms_rows(last[:, :HEAD], qg_ref[...]).astype(jnp.bfloat16)
        qbuf[p, :, :, (HEADS - 1) * HEAD :] = head.reshape(N_EXP, PR, HEAD)
        for pair in range((HEADS - 1) // 2):
            low = pair * 2 * HEAD
            raw = jnp.dot(
                xall[p], wall[:, low : low + 2 * HEAD], preferred_element_type=jnp.float32
            )
            for i in range(2):
                head = rms_rows(raw[:, i * HEAD : (i + 1) * HEAD], qg_ref[...]).astype(jnp.bfloat16)
                qbuf[p, :, :, low + i * HEAD : low + (i + 1) * HEAD] = head.reshape(N_EXP, PR, HEAD)
        pltpu.make_async_copy(qbuf.at[p], q_hbm.at[:, p], out_sem.at[2]).start()

        @pl.when(p > 0)
        def _():
            pass_halo(p - 1)

    pass_halo(PCH - 1)

    done(ex_hbm.at[pl.ds(0, N_EXP - 1)], a_send)
    done(wall.at[pl.ds(0, 15 * WA), :], w_send.at[0])
    done(wall.at[pl.ds(0, 15 * WB), :], w_send.at[1])
    done(xall.at[:, pl.ds(0, 2 * PR), :], x_send)
    done(xall.at[:, pl.ds(0, PR), :], f_send)
    done(xall.at[:, pl.ds(0, 4 * PR), :], s_send)
    done(kv_hbm.at[0, pl.ds(0, 2)], h_send)
    done(kv_hbm.at[0], hs_send)
    done(kv_hbm.at[0], hs_recv)
    store_hid.wait()
    done(kv_hbm.at[0, 0], out_sem.at[1])
    done(q_hbm, out_sem.at[2])


def exchange(residual, shared_out, expert_rows, expert_id, gate, gain, w_query, w_kv, q_gain, k_gain):
    any_space = pl.BlockSpec(memory_space=pl.ANY)
    vmem = pl.BlockSpec(memory_space=pltpu.VMEM)
    dma = pltpu.SemaphoreType.DMA
    bf16, f32 = jnp.bfloat16, jnp.float32
    return pl.pallas_call(
        exchange_kernel,
        out_shape=(
            jax.ShapeDtypeStruct((TOK, MODEL), bf16),
            jax.ShapeDtypeStruct((N_EXP, PCH, PR, HEADS * HEAD), bf16),
            jax.ShapeDtypeStruct((2, 3, N_EXP, PCH, PR, HEAD), bf16),
        ),
        in_specs=[any_space] * 3 + [vmem] * 3 + [any_space] * 2 + [vmem] * 2,
        out_specs=(any_space, any_space, any_space),
        scratch_shapes=[
            pltpu.VMEM((FCH, N_EXP * SLOTS, FW), bf16),
            pltpu.VMEM((TOK, MODEL), bf16),
            pltpu.VMEM((TOK, MODEL), bf16),
            pltpu.VMEM((TOK, MODEL), f32),
            pltpu.VMEM((TOK, MODEL), bf16),
            pltpu.VMEM((PCH, PM, MODEL), bf16),
            pltpu.VMEM((MODEL, COLS), bf16),
            pltpu.VMEM((PCH, N_EXP, PR, HEADS * HEAD), bf16),
            pltpu.VMEM((PCH, N_EXP, PR, HEAD), bf16),
            dma((4,)),
            dma,
            dma((FCH,)),
            dma((FCH,)),
            dma((2,)),
            dma((2, 4)),
            dma((2,)),
            dma,
            dma((PCH, 2)),
            dma,
            dma((PCH, 2)),
            dma,
            dma((PCH,)),
            dma,
            dma((PCH, 3)),
            dma,
            dma,
            dma((3,)),
        ],
        compiler_params=pltpu.CompilerParams(
            collective_id=0, has_side_effects=True, vmem_limit_bytes=VMEM_LIMIT
        ),
        cost_estimate=pl.CostEstimate(
            flops=2 * SHARD * MODEL * COLS, bytes_accessed=16 * 1024 * 1024, transcendentals=0
        ),
        name="exchange",
    )(residual, shared_out, expert_rows, expert_id, gate, gain, w_query, w_kv, q_gain, k_gain)


BQ = 512
BK = 512
NEG = -1e30
FACTOR = HEAD ** (-0.5) * math.log2(math.e)
SPREAD = HEAD * FACTOR * 1.01
EXPONENT_MOST = 100.0


def attention_kernel(
    doc_ref, qg_ref, kg_ref, q_ref, kv_ref, hid_hbm, out_ref, hid_out_hbm, values_t, queries_t, s_ref, m_ref, l_ref,
    acc_ref, hid, sem,
):
    c = lax.axis_index("ctx")
    qb = pl.program_id(0)
    steps = SHARD // BQ
    load_hid = pltpu.make_async_copy(hid_hbm, hid, sem.at[0])
    store_hid = pltpu.make_async_copy(hid, hid_out_hbm, sem.at[1])

    @pl.when(qb == 0)
    def _():
        load_hid.start()
        values_t[...] = kv_ref[1].T

    queries_t[...] = q_ref[...].T

    window = (c - 2) * SHARD
    q_low = pl.multiple_of(2 * SHARD + qb * BQ, BQ)
    position = q_low + lax.broadcasted_iota(jnp.int32, (1, BQ), 1)

    def starts(i, carried):
        end, first, least, most = carried
        end = end + doc_ref[i]
        first = jnp.where(end <= position, end, first)
        least = jnp.where(end <= q_low, end, least)
        most = jnp.where(end <= q_low + BQ - 1, end, most)
        return end, first, least, most

    _, first, least, most = lax.fori_loop(
        0, doc_ref.shape[0], starts,
        (0 - window, jnp.zeros((1, BQ), jnp.int32) - window, 0 - window, 0 - window),
    )
    l_ref[...] = jnp.zeros(l_ref.shape, jnp.float32)
    acc_ref[...] = jnp.zeros(acc_ref.shape, jnp.float32)

    def allowed_pairs(k_low, count, skip):
        k_position = k_low + lax.broadcasted_iota(jnp.int32, (count, BQ - skip), 0)
        return (k_position >= first[:, skip:]) & (k_position <= position[:, skip:])

    def raw_scores(k_low, count, skip, h):
        return jnp.dot(
            kv_ref[0, pl.ds(k_low, count), :], queries_t[h * HEAD : (h + 1) * HEAD, skip:],
            preferred_element_type=jnp.float32,
        )

    def add(k_low, count, skip, h, weights):
        l_ref[h, :, skip:] += jnp.sum(weights.reshape(count // 8, 8, BQ - skip), axis=0)
        return weights.astype(jnp.bfloat16)

    def mix(k_low, count, skip, h, probs):
        acc_ref[h, :, skip:] += jnp.dot(
            values_t[:, pl.ds(k_low, count)], probs, preferred_element_type=jnp.float32
        )

    def direct(k_low, count, skip, masked):
        scores = [raw_scores(k_low, count, skip, h) for h in range(HEADS)]
        probs = []
        for h in range(HEADS):
            weights = jnp.exp2(scores[h] * FACTOR)
            if masked:
                weights = jnp.where(allowed_pairs(k_low, count, skip), weights, 0.0)
            probs.append(add(k_low, count, skip, h, weights))
        for h in range(HEADS):
            mix(k_low, count, skip, h, probs[h])

    def score(k_low, count, skip, masked):
        for h in range(HEADS):
            scores = raw_scores(k_low, count, skip, h)
            if masked:
                scores = jnp.where(allowed_pairs(k_low, count, skip), scores, NEG)
            s_ref[h, pl.ds(k_low, count), skip:] = scores
            m_ref[h, :, skip:] = jnp.maximum(
                m_ref[h, :, skip:], jnp.max(scores.reshape(count // 8, 8, BQ - skip), axis=0)
            )

    def weigh(k_low, count, skip, masked):
        for h in range(HEADS):
            scores = s_ref[h, pl.ds(k_low, count), skip:].reshape(count // 8, 8, BQ - skip)
            weights = jnp.exp2(scores * FACTOR - m_ref[h, :, skip:][None])
            mix(k_low, count, skip, h, add(k_low, count, skip, h, weights.reshape(count, BQ - skip)))

    half = BK // 2
    low = jnp.minimum(least // half, q_low // half)
    odd = (q_low // half - low) % 2
    whole = (q_low - (low + odd) * half) // BK

    def all_blocks(act):
        def ahead(k_low, count):
            pl.when(k_low < most)(lambda: act(k_low, count, 0, True))
            pl.when(k_low >= most)(lambda: act(k_low, count, 0, False))

        @pl.when(odd == 1)
        def _():
            ahead(pl.multiple_of(low * half, half), half)

        @pl.loop(0, whole)
        def _(i):
            ahead(pl.multiple_of((low + odd) * half + i * BK, half), BK)

        act(q_low, half, 0, True)
        act(pl.multiple_of(q_low + half, half), half, half, True)

    bound = jnp.max(jnp.abs(qg_ref[...])) * jnp.max(jnp.abs(kg_ref[...])) * SPREAD
    in_range = bound <= EXPONENT_MOST

    @pl.when(in_range)
    def _():
        all_blocks(direct)

    @pl.when(jnp.logical_not(in_range))
    def _():
        m_ref[...] = jnp.full(m_ref.shape, NEG, jnp.float32)
        all_blocks(score)
        for h in range(HEADS):
            largest = jnp.max(m_ref[h], axis=0, keepdims=True) * FACTOR
            m_ref[h] = jnp.broadcast_to(largest, (8, BQ))
        all_blocks(weigh)

    for h in range(HEADS):
        total = jnp.sum(l_ref[h], axis=0, keepdims=True)
        out_ref[:, h * HEAD : (h + 1) * HEAD] = (acc_ref[h] / total).T.astype(jnp.bfloat16)

    @pl.when(qb == 0)
    def _():
        load_hid.wait()
        store_hid.start()

    @pl.when(qb == steps - 1)
    def _():
        store_hid.wait()


def attention(doc_lengths, q_gain, k_gain, queries, kv, hidden):
    any_space = pl.BlockSpec(memory_space=pl.ANY)
    vmem = pltpu.VMEM
    f32, bf16 = jnp.float32, jnp.bfloat16
    return pl.pallas_call(
        attention_kernel,
        grid=(SHARD // BQ,),
        out_shape=(
            jax.ShapeDtypeStruct((SHARD, HEADS * HEAD), bf16),
            jax.ShapeDtypeStruct((TOK, MODEL), bf16),
        ),
        in_specs=[
            pl.BlockSpec(memory_space=pltpu.SMEM),
            pl.BlockSpec(memory_space=vmem),
            pl.BlockSpec(memory_space=vmem),
            pl.BlockSpec((BQ, HEADS * HEAD), lambda i: (i, 0)),
            pl.BlockSpec((2, 3 * SHARD, HEAD), lambda i: (0, 0, 0)),
            any_space,
        ],
        out_specs=(pl.BlockSpec((BQ, HEADS * HEAD), lambda i: (i, 0)), any_space),
        scratch_shapes=[
            vmem((HEAD, 3 * SHARD), bf16),
            vmem((HEADS * HEAD, BQ), bf16),
            vmem((HEADS, 3 * SHARD, BQ), f32),
            vmem((HEADS, 8, BQ), f32),
            vmem((HEADS, 8, BQ), f32),
            vmem((HEADS, HEAD, BQ), f32),
            vmem((TOK, MODEL), bf16),
            pltpu.SemaphoreType.DMA((2,)),
        ],
        compiler_params=pltpu.CompilerParams(vmem_limit_bytes=VMEM_LIMIT),
        name="attention",
    )(doc_lengths, q_gain, k_gain, queries, kv, hidden)


def per_device(
    residual, shared_out, expert_out, expert_id, gate_value, doc_lengths, norm_gain, w_query,
    key_value_weight, query_gain, key_gain,
):
    hidden, queries, kv = exchange(
        residual,
        shared_out,
        expert_out.reshape(N_EXP, SLOTS, MODEL),
        expert_id.reshape(1, TOK),
        gate_value.reshape(1, TOK),
        norm_gain,
        w_query,
        key_value_weight,
        query_gain.reshape(1, HEAD),
        key_gain.reshape(1, HEAD),
    )
    attended, hidden_out = attention(
        doc_lengths,
        query_gain.reshape(1, HEAD),
        key_gain.reshape(1, HEAD),
        queries.reshape(SHARD, HEADS * HEAD),
        kv.reshape(2, 3 * SHARD, HEAD),
        hidden,
    )
    return (hidden_out, attended)


def solution(mesh):
    placed = (
        P(("ctx", "exp"), None),
        P(("ctx", "exp"), None),
        P("ctx", "exp", None, None, None, None),
        P(("ctx", "exp"), None),
        P(("ctx", "exp"), None),
        P(),
        P(),
        P("ctx", "exp"),
        P("ctx", None),
        P(),
        P(),
    )
    return jax.shard_map(
        per_device,
        mesh=mesh,
        in_specs=placed,
        out_specs=(P(("ctx", "exp"), None), P("ctx", "exp")),
        check_vma=False,
    )
```

```python
import functools
import math

import jax
import jax.numpy as jnp
from jax import lax
from jax.experimental import pallas as pl
from jax.experimental.pallas import tpu as pltpu
from jax.sharding import PartitionSpec as P

MESH = pl.DeviceIdType.MESH
MODEL = 6400
HEAD = 128
HEADS = 5
COLS = (HEADS + 1) * HEAD
TOK = 128
SHARD = 1024
N_CTX = 16
N_EXP = 8
SLOTS = 32
FCH = 5
FW = MODEL // FCH
PCH = 8
PR = TOK // PCH
AHEAD = 3
PM = N_EXP * PR
WROWS = 400
WA = 208
WB = WROWS - WA
EPS = 1e-06
VMEM_LIMIT = 56 * 1024 * 1024


def rms_rows(values, gain):
    mean_square = jnp.mean(values * values, axis=-1, keepdims=True)
    return values * lax.rsqrt(mean_square + EPS) * gain


def exchange_kernel(
    res_hbm, sh_hbm, ex_hbm, eid_ref, gate_ref, gain_ref, wq_hbm, wkv_hbm, qg_ref, kg_ref,
    hid_hbm, q_hbm, kv_hbm,
    slots, res, sh, summed, hid, xall, wall, qbuf, kvbuf,
    loc_sem, a_send, a_recv, a_own, w_send, w_recv1, w_recv2, x_send, x_recv, f_send, f_recv, s_send, s_recv,
    h_send, h_recv, hs_send, hs_recv, out_sem,
):
    c = lax.axis_index("ctx")
    e = lax.axis_index("exp")
    x, z = c // 4, c % 4
    y, k = e // 2, e % 2

    def along_x(d):
        return (((x + d) % 4) * 4 + z, e)

    def along_z(d):
        return (x * 4 + (z + d) % 4, e)

    def along_y(d):
        return (c, ((y + d) % 4) * 2 + k)

    def along_ctx(d):
        return ((c + d + N_CTX) % N_CTX, e)

    sibling = (c, y * 2 + (1 - k))

    def remote(src, dst, send, recv, to):
        pltpu.make_async_remote_copy(
            src_ref=src, dst_ref=dst, send_sem=send, recv_sem=recv, device_id=to, device_id_type=MESH
        ).start()

    def done(ref, sem):
        pltpu.make_async_copy(ref, ref, sem).wait()

    w_own = wall.at[pl.ds(pl.multiple_of(c * WROWS, 16), WROWS), :]
    load_q = pltpu.make_async_copy(wq_hbm, w_own.at[:, : HEADS * HEAD], loc_sem.at[0])
    load_q.start()
    kv_column = pl.multiple_of(e * HEAD, HEAD)
    load_kv = pltpu.make_async_copy(
        wkv_hbm.at[:, pl.ds(kv_column, HEAD)], w_own.at[:, HEADS * HEAD :], loc_sem.at[1]
    )
    load_kv.start()
    load_res = pltpu.make_async_copy(res_hbm, res, loc_sem.at[2])
    load_res.start()
    load_sh = pltpu.make_async_copy(sh_hbm, sh, loc_sem.at[3])
    load_sh.start()
    mine = pl.ds(pl.multiple_of(e * SLOTS, SLOTS), SLOTS)
    for f in range(FCH):
        pltpu.make_async_copy(
            ex_hbm.at[e, :, pl.ds(f * FW, FW)], slots.at[f, mine, :], a_own.at[f]
        ).start()

    barrier = pltpu.get_barrier_semaphore()
    for d in range(1, N_EXP):
        pl.semaphore_signal(barrier, inc=1, device_id=(c, (e + d) % N_EXP), device_id_type=MESH)
    for d in range(1, 4):
        pl.semaphore_signal(barrier, inc=1, device_id=along_x(d), device_id_type=MESH)
        pl.semaphore_signal(barrier, inc=1, device_id=along_z(d), device_id_type=MESH)
    for d in (-2, -1, 1, 2):
        pl.semaphore_signal(barrier, inc=1, device_id=along_ctx(d), device_id_type=MESH)
    pl.semaphore_wait(barrier, (N_EXP - 1) + 6 + 4)

    @pl.loop(0, FCH)
    def _(f):
        columns = pl.ds(pl.multiple_of(f * FW, 128), FW)
        for d in range(1, N_EXP):
            to = (e + d) % N_EXP
            remote(ex_hbm.at[to, :, columns], slots.at[f, mine, :], a_send, a_recv.at[f], (c, to))

    def half_a(index):
        return wall.at[pl.ds(pl.multiple_of(index * WROWS, 16), WA), :]

    def half_b(index):
        return wall.at[pl.ds(pl.multiple_of(index * WROWS + WA, 16), WB), :]

    load_q.wait()
    load_kv.wait()
    for d in (1, 3, 2):
        remote(half_a(c), half_a(c), w_send.at[0], w_recv1.at[0, d], along_x(d))
        remote(half_b(c), half_b(c), w_send.at[1], w_recv1.at[1, d], along_z(d))
    for d in (1, 3, 2):
        remote(half_a(c), half_a(c), w_send.at[0], w_recv2.at[0], along_z(d))
        remote(half_b(c), half_b(c), w_send.at[1], w_recv2.at[1], along_x(d))

    experts = 2 * N_EXP
    chosen = eid_ref[...]
    named = jnp.where(chosen == lax.broadcasted_iota(jnp.int32, (experts, TOK), 0), 1.0, 0.0)
    earlier = lax.broadcasted_iota(jnp.int32, (TOK, TOK), 0) < lax.broadcasted_iota(
        jnp.int32, (TOK, TOK), 1
    )
    before = jnp.dot(
        named.astype(jnp.bfloat16),
        jnp.where(earlier, 1.0, 0.0).astype(jnp.bfloat16),
        preferred_element_type=jnp.float32,
    )
    slot = jnp.sum(named * before, axis=0, keepdims=True)
    row = chosen.astype(jnp.float32) * float(SLOTS // 2) + slot
    place = lax.broadcasted_iota(jnp.int32, (N_EXP * SLOTS, TOK), 0).astype(jnp.float32)
    pick = jnp.where(place == row, 1.0, 0.0).T.astype(jnp.bfloat16)
    gate = jnp.broadcast_to(gate_ref[...], (TOK, TOK)).T[:, :1]

    for d in (1, 3, 2):
        done(half_a(0), w_recv1.at[0, d])
        got = ((x - d + 4) % 4) * 4 + z
        for d2 in (1, 3, 2):
            remote(half_a(got), half_a(got), w_send.at[0], w_recv2.at[0], along_z(d2))
        done(half_b(0), w_recv1.at[1, d])
        got = x * 4 + (z - d + 4) % 4
        for d2 in (1, 3, 2):
            remote(half_b(got), half_b(got), w_send.at[1], w_recv2.at[1], along_x(d2))

    load_res.wait()
    load_sh.wait()
    squares = jnp.zeros((TOK, 1), jnp.float32)
    for f in range(FCH):
        done(slots.at[f, pl.ds(0, SLOTS), :], a_own.at[f])
        done(slots.at[f, pl.ds(0, SLOTS * (N_EXP - 1)), :], a_recv.at[f])
        columns = pl.ds(f * FW, FW)
        routed = jnp.dot(pick, slots[f], preferred_element_type=jnp.float32)
        total = (
            res[:, columns].astype(jnp.float32) + sh[:, columns].astype(jnp.float32) + gate * routed
        )
        hid[:, columns] = total.astype(jnp.bfloat16)
        summed[:, columns] = total
        squares = squares + jnp.sum(total * total, axis=1, keepdims=True)
    scale = lax.rsqrt(squares * (1.0 / MODEL) + EPS)
    here = pl.ds(pl.multiple_of(e * PR, PR), PR)
    gain = gain_ref[...][None, :]
    def rows_of(p, d):
        source = ((y + d + 4) % 4) * 2 + k
        return xall.at[p, pl.ds(pl.multiple_of(source * PR, PR), PR), :]

    def send_chunk(p):
        block = rows_of(p, 0)
        remote(block, block, x_send, x_recv.at[p, 0], along_y(1))
        remote(block, block, x_send, x_recv.at[p, 1], along_y(3))
        remote(block, block, s_send, s_recv.at[p], sibling)

    for p in range(PCH):
        rows = slice(p * PR, (p + 1) * PR)
        xall[p, here, :] = (summed[rows, :] * scale[rows] * gain).astype(jnp.bfloat16)
        if p < AHEAD:
            send_chunk(p)
    store_hid = pltpu.make_async_copy(hid, hid_hbm, out_sem.at[0])
    store_hid.start()

    def half_of(p, d, side):
        return rows_of(p, d).at[:, pl.ds(side * (MODEL // 2), MODEL // 2)]

    def pass_on(p):
        for side, d in ((0, -1), (1, 1)):
            done(rows_of(p, d), x_recv.at[p, side])
            part = half_of(p, d, side)
            remote(part, part, f_send, f_recv.at[p, side], along_y(-d))
        for d in (-1, 1):
            block = rows_of(p, d)
            remote(block, block, s_send, s_recv.at[p], sibling)

        @pl.when(p < PCH - AHEAD)
        def _():
            send_chunk(p + AHEAD)

    @pl.loop(0, PCH // 2)
    def _(p):
        pass_on(p)

    done(wall.at[pl.ds(0, 12 * WA), :], w_recv2.at[0])
    done(wall.at[pl.ds(0, 12 * WB), :], w_recv2.at[1])

    def pass_halo(p):
        for dist in (1, 2):
            part = kv_hbm.at[k, 2 - dist, :, p]
            done(part, h_recv.at[p, dist])
            remote(part, part, hs_send, hs_recv, sibling)

    @pl.loop(0, PCH)
    def _(p):
        @pl.when((p >= PCH // 2 - 2) & (p < PCH - 2))
        def _():
            pass_on(p + 2)

        for side in range(2):
            done(half_of(p, 2, side), f_recv.at[p, side])
        block = rows_of(p, 2)
        remote(block, block, s_send, s_recv.at[p], sibling)
        done(xall.at[p, pl.ds(0, 4 * PR), :], s_recv.at[p])

        last = jnp.dot(
            xall[p], wall[:, (HEADS - 1) * HEAD :], preferred_element_type=jnp.float32
        )
        raw = last[:, HEAD:]
        part = jnp.where(k == 0, rms_rows(raw, kg_ref[...]), raw).astype(jnp.bfloat16)
        kvbuf[p] = part.reshape(N_EXP, PR, HEAD)
        for dist in (2, 1):
            remote(
                kvbuf.at[p], kv_hbm.at[k, 2 - dist, :, p], h_send, h_recv.at[p, dist], along_ctx(dist)
            )
        remote(kvbuf.at[p], kv_hbm.at[k, 2, :, p], hs_send, hs_recv, sibling)
        pltpu.make_async_copy(kvbuf.at[p], kv_hbm.at[k, 2, :, p], out_sem.at[1]).start()
        head = rms_rows(last[:, :HEAD], qg_ref[...]).astype(jnp.bfloat16)
        qbuf[p, :, :, (HEADS - 1) * HEAD :] = head.reshape(N_EXP, PR, HEAD)
        for pair in range((HEADS - 1) // 2):
            low = pair * 2 * HEAD
            raw = jnp.dot(
                xall[p], wall[:, low : low + 2 * HEAD], preferred_element_type=jnp.float32
            )
            for i in range(2):
                head = rms_rows(raw[:, i * HEAD : (i + 1) * HEAD], qg_ref[...]).astype(jnp.bfloat16)
                qbuf[p, :, :, low + i * HEAD : low + (i + 1) * HEAD] = head.reshape(N_EXP, PR, HEAD)
        pltpu.make_async_copy(qbuf.at[p], q_hbm.at[:, p], out_sem.at[2]).start()

        @pl.when(p > 0)
        def _():
            pass_halo(p - 1)

    pass_halo(PCH - 1)

    done(ex_hbm.at[pl.ds(0, N_EXP - 1)], a_send)
    done(wall.at[pl.ds(0, 15 * WA), :], w_send.at[0])
    done(wall.at[pl.ds(0, 15 * WB), :], w_send.at[1])
    done(xall.at[:, pl.ds(0, 2 * PR), :], x_send)
    done(xall.at[:, pl.ds(0, PR), :], f_send)
    done(xall.at[:, pl.ds(0, 4 * PR), :], s_send)
    done(kv_hbm.at[0, pl.ds(0, 2)], h_send)
    done(kv_hbm.at[0], hs_send)
    done(kv_hbm.at[0], hs_recv)
    store_hid.wait()
    done(kv_hbm.at[0, 0], out_sem.at[1])
    done(q_hbm, out_sem.at[2])


def exchange(residual, shared_out, expert_rows, expert_id, gate, gain, w_query, w_kv, q_gain, k_gain):
    any_space = pl.BlockSpec(memory_space=pl.ANY)
    vmem = pl.BlockSpec(memory_space=pltpu.VMEM)
    dma = pltpu.SemaphoreType.DMA
    bf16, f32 = jnp.bfloat16, jnp.float32
    return pl.pallas_call(
        exchange_kernel,
        out_shape=(
            jax.ShapeDtypeStruct((TOK, MODEL), bf16),
            jax.ShapeDtypeStruct((N_EXP, PCH, PR, HEADS * HEAD), bf16),
            jax.ShapeDtypeStruct((2, 3, N_EXP, PCH, PR, HEAD), bf16),
        ),
        in_specs=[any_space] * 3 + [vmem] * 3 + [any_space] * 2 + [vmem] * 2,
        out_specs=(any_space, any_space, any_space),
        scratch_shapes=[
            pltpu.VMEM((FCH, N_EXP * SLOTS, FW), bf16),
            pltpu.VMEM((TOK, MODEL), bf16),
            pltpu.VMEM((TOK, MODEL), bf16),
            pltpu.VMEM((TOK, MODEL), f32),
            pltpu.VMEM((TOK, MODEL), bf16),
            pltpu.VMEM((PCH, PM, MODEL), bf16),
            pltpu.VMEM((MODEL, COLS), bf16),
            pltpu.VMEM((PCH, N_EXP, PR, HEADS * HEAD), bf16),
            pltpu.VMEM((PCH, N_EXP, PR, HEAD), bf16),
            dma((4,)),
            dma,
            dma((FCH,)),
            dma((FCH,)),
            dma((2,)),
            dma((2, 4)),
            dma((2,)),
            dma,
            dma((PCH, 2)),
            dma,
            dma((PCH, 2)),
            dma,
            dma((PCH,)),
            dma,
            dma((PCH, 3)),
            dma,
            dma,
            dma((3,)),
        ],
        compiler_params=pltpu.CompilerParams(
            collective_id=0, has_side_effects=True, vmem_limit_bytes=VMEM_LIMIT
        ),
        cost_estimate=pl.CostEstimate(
            flops=2 * SHARD * MODEL * COLS, bytes_accessed=16 * 1024 * 1024, transcendentals=0
        ),
        name="exchange",
    )(residual, shared_out, expert_rows, expert_id, gate, gain, w_query, w_kv, q_gain, k_gain)


BQ = 512
BK = 512
NEG = -1e30
FACTOR = HEAD ** (-0.5) * math.log2(math.e)
SPREAD = HEAD * FACTOR * 1.01
EXPONENT_MOST = 100.0


def attention_kernel(
    doc_ref, qg_ref, kg_ref, q_ref, kv_ref, hid_hbm, out_ref, hid_out_hbm, values_t, queries_t, s_ref, m_ref, l_ref,
    acc_ref, keep_ref, hid, sem,
):
    c = lax.axis_index("ctx")
    qb = pl.program_id(0)
    steps = SHARD // BQ
    load_hid = pltpu.make_async_copy(hid_hbm, hid, sem.at[0])
    store_hid = pltpu.make_async_copy(hid, hid_out_hbm, sem.at[1])

    @pl.when(qb == 0)
    def _():
        load_hid.start()
        values_t[...] = kv_ref[1].T

    queries_t[...] = q_ref[...].T

    window = (c - 2) * SHARD
    q_low = pl.multiple_of(2 * SHARD + qb * BQ, BQ)
    position = q_low + lax.broadcasted_iota(jnp.int32, (1, BQ), 1)

    def starts(i, carried):
        end, first, least, most = carried
        end = end + doc_ref[i]
        first = jnp.where(end <= position, end, first)
        least = jnp.where(end <= q_low, end, least)
        most = jnp.where(end <= q_low + BQ - 1, end, most)
        return end, first, least, most

    _, first, least, most = lax.fori_loop(
        0, doc_ref.shape[0], starts,
        (0 - window, jnp.zeros((1, BQ), jnp.int32) - window, 0 - window, 0 - window),
    )
    l_ref[...] = jnp.zeros(l_ref.shape, jnp.float32)
    acc_ref[...] = jnp.zeros(acc_ref.shape, jnp.float32)

    def allowed_pairs(k_low, count, skip):
        k_position = k_low + lax.broadcasted_iota(jnp.int32, (count, BQ - skip), 0)
        return (k_position >= first[:, skip:]) & (k_position <= position[:, skip:])

    def raw_scores(k_low, count, skip, h):
        return jnp.dot(
            kv_ref[0, pl.ds(k_low, count), :], queries_t[h * HEAD : (h + 1) * HEAD, skip:],
            preferred_element_type=jnp.float32,
        )

    def add(k_low, count, skip, h, weights):
        l_ref[h, :, skip:] += jnp.sum(weights.reshape(count // 8, 8, BQ - skip), axis=0)
        return weights.astype(jnp.bfloat16)

    def mix(k_low, count, skip, h, probs):
        acc_ref[h, :, skip:] += jnp.dot(
            values_t[:, pl.ds(k_low, count)], probs, preferred_element_type=jnp.float32
        )

    def direct(*parts):
        at = 0
        for k_low, count, skip, masked in parts:
            if masked:
                keep = jnp.where(allowed_pairs(k_low, count, skip), 1.0, 0.0)
                keep_ref[at : at + count, skip:] = keep
            at += count
        scores = [
            [raw_scores(k_low, count, skip, h) for h in range(HEADS)]
            for k_low, count, skip, _ in parts
        ]
        probs = []
        at = 0
        for i, (k_low, count, skip, masked) in enumerate(parts):
            for h in range(HEADS):
                weights = jnp.exp2(scores[i][h] * FACTOR)
                if masked:
                    weights = weights * keep_ref[at : at + count, skip:]
                probs.append(add(k_low, count, skip, h, weights))
            at += count
        for i, (k_low, count, skip, _) in enumerate(parts):
            for h in range(HEADS):
                mix(k_low, count, skip, h, probs[i * HEADS + h])

    def score(*parts):
        for part in parts:
            score_part(*part)

    def score_part(k_low, count, skip, masked):
        for h in range(HEADS):
            scores = raw_scores(k_low, count, skip, h)
            if masked:
                scores = jnp.where(allowed_pairs(k_low, count, skip), scores, NEG)
            s_ref[h, pl.ds(k_low, count), skip:] = scores
            m_ref[h, :, skip:] = jnp.maximum(
                m_ref[h, :, skip:], jnp.max(scores.reshape(count // 8, 8, BQ - skip), axis=0)
            )

    def weigh(*parts):
        for part in parts:
            weigh_part(*part)

    def weigh_part(k_low, count, skip, masked):
        for h in range(HEADS):
            scores = s_ref[h, pl.ds(k_low, count), skip:].reshape(count // 8, 8, BQ - skip)
            weights = jnp.exp2(scores * FACTOR - m_ref[h, :, skip:][None])
            mix(k_low, count, skip, h, add(k_low, count, skip, h, weights.reshape(count, BQ - skip)))

    half = BK // 2
    low = jnp.minimum(least // half, q_low // half)
    odd = (q_low // half - low) % 2
    whole = (q_low - (low + odd) * half) // BK

    def all_blocks(act):
        def ahead(k_low, count):
            pl.when(k_low < most)(lambda: act((k_low, count, 0, True)))
            pl.when(k_low >= most)(lambda: act((k_low, count, 0, False)))

        @pl.when(odd == 1)
        def _():
            ahead(pl.multiple_of(low * half, half), half)

        @pl.loop(0, whole)
        def _(i):
            ahead(pl.multiple_of((low + odd) * half + i * BK, half), BK)

        act((q_low, half, 0, True), (pl.multiple_of(q_low + half, half), half, half, True))

    bound = jnp.max(jnp.abs(qg_ref[...])) * jnp.max(jnp.abs(kg_ref[...])) * SPREAD
    in_range = bound <= EXPONENT_MOST

    @pl.when(in_range)
    def _():
        all_blocks(direct)

    @pl.when(jnp.logical_not(in_range))
    def _():
        m_ref[...] = jnp.full(m_ref.shape, NEG, jnp.float32)
        all_blocks(score)
        for h in range(HEADS):
            largest = jnp.max(m_ref[h], axis=0, keepdims=True) * FACTOR
            m_ref[h] = jnp.broadcast_to(largest, (8, BQ))
        all_blocks(weigh)

    for h in range(HEADS):
        total = jnp.sum(l_ref[h], axis=0, keepdims=True)
        out_ref[:, h * HEAD : (h + 1) * HEAD] = (acc_ref[h] / total).T.astype(jnp.bfloat16)

    @pl.when(qb == 0)
    def _():
        load_hid.wait()
        store_hid.start()

    @pl.when(qb == steps - 1)
    def _():
        store_hid.wait()


def attention(doc_lengths, q_gain, k_gain, queries, kv, hidden):
    any_space = pl.BlockSpec(memory_space=pl.ANY)
    vmem = pltpu.VMEM
    f32, bf16 = jnp.float32, jnp.bfloat16
    return pl.pallas_call(
        attention_kernel,
        grid=(SHARD // BQ,),
        out_shape=(
            jax.ShapeDtypeStruct((SHARD, HEADS * HEAD), bf16),
            jax.ShapeDtypeStruct((TOK, MODEL), bf16),
        ),
        in_specs=[
            pl.BlockSpec(memory_space=pltpu.SMEM),
            pl.BlockSpec(memory_space=vmem),
            pl.BlockSpec(memory_space=vmem),
            pl.BlockSpec((BQ, HEADS * HEAD), lambda i: (i, 0)),
            pl.BlockSpec((2, 3 * SHARD, HEAD), lambda i: (0, 0, 0)),
            any_space,
        ],
        out_specs=(pl.BlockSpec((BQ, HEADS * HEAD), lambda i: (i, 0)), any_space),
        scratch_shapes=[
            vmem((HEAD, 3 * SHARD), bf16),
            vmem((HEADS * HEAD, BQ), bf16),
            vmem((HEADS, 3 * SHARD, BQ), f32),
            vmem((HEADS, 8, BQ), f32),
            vmem((HEADS, 8, BQ), f32),
            vmem((HEADS, HEAD, BQ), f32),
            vmem((BK, BQ), f32),
            vmem((TOK, MODEL), bf16),
            pltpu.SemaphoreType.DMA((2,)),
        ],
        compiler_params=pltpu.CompilerParams(vmem_limit_bytes=VMEM_LIMIT),
        name="attention",
    )(doc_lengths, q_gain, k_gain, queries, kv, hidden)


def per_device(
    residual, shared_out, expert_out, expert_id, gate_value, doc_lengths, norm_gain, w_query,
    key_value_weight, query_gain, key_gain,
):
    hidden, queries, kv = exchange(
        residual,
        shared_out,
        expert_out.reshape(N_EXP, SLOTS, MODEL),
        expert_id.reshape(1, TOK),
        gate_value.reshape(1, TOK),
        norm_gain,
        w_query,
        key_value_weight,
        query_gain.reshape(1, HEAD),
        key_gain.reshape(1, HEAD),
    )
    attended, hidden_out = attention(
        doc_lengths,
        query_gain.reshape(1, HEAD),
        key_gain.reshape(1, HEAD),
        queries.reshape(SHARD, HEADS * HEAD),
        kv.reshape(2, 3 * SHARD, HEAD),
        hidden,
    )
    return (hidden_out, attended)


def solution(mesh):
    placed = (
        P(("ctx", "exp"), None),
        P(("ctx", "exp"), None),
        P("ctx", "exp", None, None, None, None),
        P(("ctx", "exp"), None),
        P(("ctx", "exp"), None),
        P(),
        P(),
        P("ctx", "exp"),
        P("ctx", None),
        P(),
        P(),
    )
    return jax.shard_map(
        per_device,
        mesh=mesh,
        in_specs=placed,
        out_specs=(P(("ctx", "exp"), None), P("ctx", "exp")),
        check_vma=False,
    )
```

```python
import functools
import math

import jax
import jax.numpy as jnp
from jax import lax
from jax.experimental import pallas as pl
from jax.experimental.pallas import tpu as pltpu
from jax.sharding import PartitionSpec as P

MESH = pl.DeviceIdType.MESH
MODEL = 6400
HEAD = 128
HEADS = 5
COLS = (HEADS + 1) * HEAD
TOK = 128
SHARD = 1024
N_CTX = 16
N_EXP = 8
SLOTS = 32
FCH = 5
FW = MODEL // FCH
PCH = 8
PR = TOK // PCH
AHEAD = 3
PM = N_EXP * PR
WROWS = 400
WA = 208
WB = WROWS - WA
EPS = 1e-06
VMEM_LIMIT = 56 * 1024 * 1024


def rms_rows(values, gain):
    mean_square = jnp.mean(values * values, axis=-1, keepdims=True)
    return values * lax.rsqrt(mean_square + EPS) * gain


def exchange_kernel(
    res_hbm, sh_hbm, ex_hbm, eid_ref, gate_ref, gain_ref, wq_hbm, wkv_hbm, qg_ref, kg_ref,
    hid_hbm, q_hbm, kv_hbm,
    slots, res, sh, summed, hid, xall, wall, qbuf, kvbuf,
    loc_sem, a_send, a_recv, a_own, w_send, w_recv1, w_recv2, x_send, x_recv, f_send, f_recv, s_send, s_recv,
    h_send, h_recv, hs_send, hs_recv, out_sem,
):
    c = lax.axis_index("ctx")
    e = lax.axis_index("exp")
    x, z = c // 4, c % 4
    y, k = e // 2, e % 2

    def along_x(d):
        return (((x + d) % 4) * 4 + z, e)

    def along_z(d):
        return (x * 4 + (z + d) % 4, e)

    def along_y(d):
        return (c, ((y + d) % 4) * 2 + k)

    def along_ctx(d):
        return ((c + d + N_CTX) % N_CTX, e)

    sibling = (c, y * 2 + (1 - k))

    def remote(src, dst, send, recv, to):
        pltpu.make_async_remote_copy(
            src_ref=src, dst_ref=dst, send_sem=send, recv_sem=recv, device_id=to, device_id_type=MESH
        ).start()

    def done(ref, sem):
        pltpu.make_async_copy(ref, ref, sem).wait()

    w_own = wall.at[pl.ds(pl.multiple_of(c * WROWS, 16), WROWS), :]
    load_q = pltpu.make_async_copy(wq_hbm, w_own.at[:, : HEADS * HEAD], loc_sem.at[0])
    load_q.start()
    kv_column = pl.multiple_of(e * HEAD, HEAD)
    load_kv = pltpu.make_async_copy(
        wkv_hbm.at[:, pl.ds(kv_column, HEAD)], w_own.at[:, HEADS * HEAD :], loc_sem.at[1]
    )
    load_kv.start()
    load_res = pltpu.make_async_copy(res_hbm, res, loc_sem.at[2])
    load_res.start()
    load_sh = pltpu.make_async_copy(sh_hbm, sh, loc_sem.at[3])
    load_sh.start()
    mine = pl.ds(pl.multiple_of(e * SLOTS, SLOTS), SLOTS)
    for f in range(FCH):
        pltpu.make_async_copy(
            ex_hbm.at[e, :, pl.ds(f * FW, FW)], slots.at[f, mine, :], a_own.at[f]
        ).start()

    barrier = pltpu.get_barrier_semaphore()
    for d in range(1, N_EXP):
        pl.semaphore_signal(barrier, inc=1, device_id=(c, (e + d) % N_EXP), device_id_type=MESH)
    for d in range(1, 4):
        pl.semaphore_signal(barrier, inc=1, device_id=along_x(d), device_id_type=MESH)
        pl.semaphore_signal(barrier, inc=1, device_id=along_z(d), device_id_type=MESH)
    for d in (-2, -1, 1, 2):
        pl.semaphore_signal(barrier, inc=1, device_id=along_ctx(d), device_id_type=MESH)
    pl.semaphore_wait(barrier, (N_EXP - 1) + 6 + 4)

    @pl.loop(0, FCH)
    def _(f):
        columns = pl.ds(pl.multiple_of(f * FW, 128), FW)
        for d in range(1, N_EXP):
            to = (e + d) % N_EXP
            remote(ex_hbm.at[to, :, columns], slots.at[f, mine, :], a_send, a_recv.at[f], (c, to))

    def half_a(index):
        return wall.at[pl.ds(pl.multiple_of(index * WROWS, 16), WA), :]

    def half_b(index):
        return wall.at[pl.ds(pl.multiple_of(index * WROWS + WA, 16), WB), :]

    load_q.wait()
    load_kv.wait()
    for d in (1, 3, 2):
        remote(half_a(c), half_a(c), w_send.at[0], w_recv1.at[0, d], along_x(d))
        remote(half_b(c), half_b(c), w_send.at[1], w_recv1.at[1, d], along_z(d))
    for d in (1, 3, 2):
        remote(half_a(c), half_a(c), w_send.at[0], w_recv2.at[0], along_z(d))
        remote(half_b(c), half_b(c), w_send.at[1], w_recv2.at[1], along_x(d))

    experts = 2 * N_EXP
    chosen = eid_ref[...]
    named = jnp.where(chosen == lax.broadcasted_iota(jnp.int32, (experts, TOK), 0), 1.0, 0.0)
    earlier = lax.broadcasted_iota(jnp.int32, (TOK, TOK), 0) < lax.broadcasted_iota(
        jnp.int32, (TOK, TOK), 1
    )
    before = jnp.dot(
        named.astype(jnp.bfloat16),
        jnp.where(earlier, 1.0, 0.0).astype(jnp.bfloat16),
        preferred_element_type=jnp.float32,
    )
    slot = jnp.sum(named * before, axis=0, keepdims=True)
    row = chosen.astype(jnp.float32) * float(SLOTS // 2) + slot
    place = lax.broadcasted_iota(jnp.int32, (N_EXP * SLOTS, TOK), 0).astype(jnp.float32)
    pick = jnp.where(place == row, 1.0, 0.0).T.astype(jnp.bfloat16)
    gate = jnp.broadcast_to(gate_ref[...], (TOK, TOK)).T[:, :1]

    for d in (1, 3, 2):
        done(half_a(0), w_recv1.at[0, d])
        got = ((x - d + 4) % 4) * 4 + z
        for d2 in (1, 3, 2):
            remote(half_a(got), half_a(got), w_send.at[0], w_recv2.at[0], along_z(d2))
        done(half_b(0), w_recv1.at[1, d])
        got = x * 4 + (z - d + 4) % 4
        for d2 in (1, 3, 2):
            remote(half_b(got), half_b(got), w_send.at[1], w_recv2.at[1], along_x(d2))

    load_res.wait()
    load_sh.wait()
    squares = jnp.zeros((TOK, 1), jnp.float32)
    for f in range(FCH):
        done(slots.at[f, pl.ds(0, SLOTS), :], a_own.at[f])
        done(slots.at[f, pl.ds(0, SLOTS * (N_EXP - 1)), :], a_recv.at[f])
        columns = pl.ds(f * FW, FW)
        routed = jnp.dot(pick, slots[f], preferred_element_type=jnp.float32)
        total = (
            res[:, columns].astype(jnp.float32) + sh[:, columns].astype(jnp.float32) + gate * routed
        )
        hid[:, columns] = total.astype(jnp.bfloat16)
        summed[:, columns] = total
        squares = squares + jnp.sum(total * total, axis=1, keepdims=True)
    scale = lax.rsqrt(squares * (1.0 / MODEL) + EPS)
    here = pl.ds(pl.multiple_of(e * PR, PR), PR)
    gain = gain_ref[...][None, :]
    def rows_of(p, d):
        source = ((y + d + 4) % 4) * 2 + k
        return xall.at[p, pl.ds(pl.multiple_of(source * PR, PR), PR), :]

    def send_chunk(p):
        block = rows_of(p, 0)
        remote(block, block, x_send, x_recv.at[p, 0], along_y(1))
        remote(block, block, x_send, x_recv.at[p, 1], along_y(3))
        remote(block, block, s_send, s_recv.at[p], sibling)

    for p in range(PCH):
        rows = slice(p * PR, (p + 1) * PR)
        xall[p, here, :] = (summed[rows, :] * scale[rows] * gain).astype(jnp.bfloat16)
        if p < AHEAD:
            send_chunk(p)
    store_hid = pltpu.make_async_copy(hid, hid_hbm, out_sem.at[0])
    store_hid.start()

    def half_of(p, d, side):
        return rows_of(p, d).at[:, pl.ds(side * (MODEL // 2), MODEL // 2)]

    def pass_on(p):
        for side, d in ((0, -1), (1, 1)):
            done(rows_of(p, d), x_recv.at[p, side])
            part = half_of(p, d, side)
            remote(part, part, f_send, f_recv.at[p, side], along_y(-d))
        for d in (-1, 1):
            block = rows_of(p, d)
            remote(block, block, s_send, s_recv.at[p], sibling)

        @pl.when(p < PCH - AHEAD)
        def _():
            send_chunk(p + AHEAD)

    @pl.loop(0, PCH // 2)
    def _(p):
        pass_on(p)

    done(wall.at[pl.ds(0, 12 * WA), :], w_recv2.at[0])
    done(wall.at[pl.ds(0, 12 * WB), :], w_recv2.at[1])

    def pass_halo(p):
        for dist in (1, 2):
            part = kv_hbm.at[k, 2 - dist, :, p]
            done(part, h_recv.at[p, dist])
            remote(part, part, hs_send, hs_recv, sibling)

    @pl.loop(0, PCH)
    def _(p):
        @pl.when((p >= PCH // 2 - 2) & (p < PCH - 2))
        def _():
            pass_on(p + 2)

        for side in range(2):
            done(half_of(p, 2, side), f_recv.at[p, side])
        block = rows_of(p, 2)
        remote(block, block, s_send, s_recv.at[p], sibling)
        done(xall.at[p, pl.ds(0, 4 * PR), :], s_recv.at[p])

        last = jnp.dot(
            xall[p], wall[:, (HEADS - 1) * HEAD :], preferred_element_type=jnp.float32
        )
        raw = last[:, HEAD:]
        part = jnp.where(k == 0, rms_rows(raw, kg_ref[...]), raw).astype(jnp.bfloat16)
        kvbuf[p] = part.reshape(N_EXP, PR, HEAD)
        for dist in (2, 1):
            remote(
                kvbuf.at[p], kv_hbm.at[k, 2 - dist, :, p], h_send, h_recv.at[p, dist], along_ctx(dist)
            )
        remote(kvbuf.at[p], kv_hbm.at[k, 2, :, p], hs_send, hs_recv, sibling)
        pltpu.make_async_copy(kvbuf.at[p], kv_hbm.at[k, 2, :, p], out_sem.at[1]).start()
        head = rms_rows(last[:, :HEAD], qg_ref[...]).astype(jnp.bfloat16)
        qbuf[p, :, :, (HEADS - 1) * HEAD :] = head.reshape(N_EXP, PR, HEAD)
        for pair in range((HEADS - 1) // 2):
            low = pair * 2 * HEAD
            raw = jnp.dot(
                xall[p], wall[:, low : low + 2 * HEAD], preferred_element_type=jnp.float32
            )
            for i in range(2):
                head = rms_rows(raw[:, i * HEAD : (i + 1) * HEAD], qg_ref[...]).astype(jnp.bfloat16)
                qbuf[p, :, :, low + i * HEAD : low + (i + 1) * HEAD] = head.reshape(N_EXP, PR, HEAD)
        pltpu.make_async_copy(qbuf.at[p], q_hbm.at[:, p], out_sem.at[2]).start()

        @pl.when(p > 1)
        def _():
            pass_halo(p - 2)

    pass_halo(PCH - 2)
    pass_halo(PCH - 1)

    done(ex_hbm.at[pl.ds(0, N_EXP - 1)], a_send)
    done(wall.at[pl.ds(0, 15 * WA), :], w_send.at[0])
    done(wall.at[pl.ds(0, 15 * WB), :], w_send.at[1])
    done(xall.at[:, pl.ds(0, 2 * PR), :], x_send)
    done(xall.at[:, pl.ds(0, PR), :], f_send)
    done(xall.at[:, pl.ds(0, 4 * PR), :], s_send)
    done(kv_hbm.at[0, pl.ds(0, 2)], h_send)
    done(kv_hbm.at[0], hs_send)
    done(kv_hbm.at[0], hs_recv)
    store_hid.wait()
    done(kv_hbm.at[0, 0], out_sem.at[1])
    done(q_hbm, out_sem.at[2])


def exchange(residual, shared_out, expert_rows, expert_id, gate, gain, w_query, w_kv, q_gain, k_gain):
    any_space = pl.BlockSpec(memory_space=pl.ANY)
    vmem = pl.BlockSpec(memory_space=pltpu.VMEM)
    dma = pltpu.SemaphoreType.DMA
    bf16, f32 = jnp.bfloat16, jnp.float32
    return pl.pallas_call(
        exchange_kernel,
        out_shape=(
            jax.ShapeDtypeStruct((TOK, MODEL), bf16),
            jax.ShapeDtypeStruct((N_EXP, PCH, PR, HEADS * HEAD), bf16),
            jax.ShapeDtypeStruct((2, 3, N_EXP, PCH, PR, HEAD), bf16),
        ),
        in_specs=[any_space] * 3 + [vmem] * 3 + [any_space] * 2 + [vmem] * 2,
        out_specs=(any_space, any_space, any_space),
        scratch_shapes=[
            pltpu.VMEM((FCH, N_EXP * SLOTS, FW), bf16),
            pltpu.VMEM((TOK, MODEL), bf16),
            pltpu.VMEM((TOK, MODEL), bf16),
            pltpu.VMEM((TOK, MODEL), f32),
            pltpu.VMEM((TOK, MODEL), bf16),
            pltpu.VMEM((PCH, PM, MODEL), bf16),
            pltpu.VMEM((MODEL, COLS), bf16),
            pltpu.VMEM((PCH, N_EXP, PR, HEADS * HEAD), bf16),
            pltpu.VMEM((PCH, N_EXP, PR, HEAD), bf16),
            dma((4,)),
            dma,
            dma((FCH,)),
            dma((FCH,)),
            dma((2,)),
            dma((2, 4)),
            dma((2,)),
            dma,
            dma((PCH, 2)),
            dma,
            dma((PCH, 2)),
            dma,
            dma((PCH,)),
            dma,
            dma((PCH, 3)),
            dma,
            dma,
            dma((3,)),
        ],
        compiler_params=pltpu.CompilerParams(
            collective_id=0, has_side_effects=True, vmem_limit_bytes=VMEM_LIMIT
        ),
        cost_estimate=pl.CostEstimate(
            flops=2 * SHARD * MODEL * COLS, bytes_accessed=16 * 1024 * 1024, transcendentals=0
        ),
        name="exchange",
    )(residual, shared_out, expert_rows, expert_id, gate, gain, w_query, w_kv, q_gain, k_gain)


BQ = 512
BK = 512
NEG = -1e30
FACTOR = HEAD ** (-0.5) * math.log2(math.e)
SPREAD = HEAD * FACTOR * 1.01
EXPONENT_MOST = 100.0


def attention_kernel(
    doc_ref, qg_ref, kg_ref, q_ref, kv_ref, hid_hbm, out_ref, hid_out_hbm, values_t, queries_t, s_ref, m_ref, l_ref,
    acc_ref, keep_ref, hid, sem,
):
    c = lax.axis_index("ctx")
    qb = pl.program_id(0)
    steps = SHARD // BQ
    load_hid = pltpu.make_async_copy(hid_hbm, hid, sem.at[0])
    store_hid = pltpu.make_async_copy(hid, hid_out_hbm, sem.at[1])

    @pl.when(qb == 0)
    def _():
        load_hid.start()
        values_t[...] = kv_ref[1].T

    queries_t[...] = q_ref[...].T

    window = (c - 2) * SHARD
    q_low = pl.multiple_of(2 * SHARD + qb * BQ, BQ)
    position = q_low + lax.broadcasted_iota(jnp.int32, (1, BQ), 1)

    def starts(i, carried):
        end, first, least, most = carried
        end = end + doc_ref[i]
        first = jnp.where(end <= position, end, first)
        least = jnp.where(end <= q_low, end, least)
        most = jnp.where(end <= q_low + BQ - 1, end, most)
        return end, first, least, most

    _, first, least, most = lax.fori_loop(
        0, doc_ref.shape[0], starts,
        (0 - window, jnp.zeros((1, BQ), jnp.int32) - window, 0 - window, 0 - window),
    )
    l_ref[...] = jnp.zeros(l_ref.shape, jnp.float32)
    acc_ref[...] = jnp.zeros(acc_ref.shape, jnp.float32)

    def allowed_pairs(k_low, count, skip):
        k_position = k_low + lax.broadcasted_iota(jnp.int32, (count, BQ - skip), 0)
        return (k_position >= first[:, skip:]) & (k_position <= position[:, skip:])

    def raw_scores(k_low, count, skip, h):
        return jnp.dot(
            kv_ref[0, pl.ds(k_low, count), :], queries_t[h * HEAD : (h + 1) * HEAD, skip:],
            preferred_element_type=jnp.float32,
        )

    def add(k_low, count, skip, h, weights):
        l_ref[h, :, skip:] += jnp.sum(weights.reshape(count // 8, 8, BQ - skip), axis=0)
        return weights.astype(jnp.bfloat16)

    def mix(k_low, count, skip, h, probs):
        acc_ref[h, :, skip:] += jnp.dot(
            values_t[:, pl.ds(k_low, count)], probs, preferred_element_type=jnp.float32
        )

    def direct(*parts):
        at = 0
        for k_low, count, skip, masked in parts:
            if masked:
                keep = jnp.where(allowed_pairs(k_low, count, skip), 1.0, 0.0)
                keep_ref[at : at + count, skip:] = keep
            at += count
        scores = [
            [raw_scores(k_low, count, skip, h) for h in range(HEADS)]
            for k_low, count, skip, _ in parts
        ]
        probs = []
        at = 0
        for i, (k_low, count, skip, masked) in enumerate(parts):
            for h in range(HEADS):
                weights = jnp.exp2(scores[i][h] * FACTOR)
                if masked:
                    weights = weights * keep_ref[at : at + count, skip:]
                probs.append(add(k_low, count, skip, h, weights))
            at += count
        for i, (k_low, count, skip, _) in enumerate(parts):
            for h in range(HEADS):
                mix(k_low, count, skip, h, probs[i * HEADS + h])

    def score(*parts):
        for part in parts:
            score_part(*part)

    def score_part(k_low, count, skip, masked):
        for h in range(HEADS):
            scores = raw_scores(k_low, count, skip, h)
            if masked:
                scores = jnp.where(allowed_pairs(k_low, count, skip), scores, NEG)
            s_ref[h, pl.ds(k_low, count), skip:] = scores
            m_ref[h, :, skip:] = jnp.maximum(
                m_ref[h, :, skip:], jnp.max(scores.reshape(count // 8, 8, BQ - skip), axis=0)
            )

    def weigh(*parts):
        for part in parts:
            weigh_part(*part)

    def weigh_part(k_low, count, skip, masked):
        for h in range(HEADS):
            scores = s_ref[h, pl.ds(k_low, count), skip:].reshape(count // 8, 8, BQ - skip)
            weights = jnp.exp2(scores * FACTOR - m_ref[h, :, skip:][None])
            mix(k_low, count, skip, h, add(k_low, count, skip, h, weights.reshape(count, BQ - skip)))

    half = BK // 2
    low = jnp.minimum(least // half, q_low // half)
    odd = (q_low // half - low) % 2
    whole = (q_low - (low + odd) * half) // BK

    def all_blocks(act):
        def ahead(k_low, count):
            pl.when(k_low < most)(lambda: act((k_low, count, 0, True)))
            pl.when(k_low >= most)(lambda: act((k_low, count, 0, False)))

        @pl.when(odd == 1)
        def _():
            ahead(pl.multiple_of(low * half, half), half)

        @pl.loop(0, whole)
        def _(i):
            ahead(pl.multiple_of((low + odd) * half + i * BK, half), BK)

        act((q_low, half, 0, True), (pl.multiple_of(q_low + half, half), half, half, True))

    bound = jnp.max(jnp.abs(qg_ref[...])) * jnp.max(jnp.abs(kg_ref[...])) * SPREAD
    in_range = bound <= EXPONENT_MOST

    @pl.when(in_range)
    def _():
        all_blocks(direct)

    @pl.when(jnp.logical_not(in_range))
    def _():
        m_ref[...] = jnp.full(m_ref.shape, NEG, jnp.float32)
        all_blocks(score)
        for h in range(HEADS):
            largest = jnp.max(m_ref[h], axis=0, keepdims=True) * FACTOR
            m_ref[h] = jnp.broadcast_to(largest, (8, BQ))
        all_blocks(weigh)

    for h in range(HEADS):
        total = jnp.sum(l_ref[h], axis=0, keepdims=True)
        out_ref[:, h * HEAD : (h + 1) * HEAD] = (acc_ref[h] / total).T.astype(jnp.bfloat16)

    @pl.when(qb == 0)
    def _():
        load_hid.wait()
        store_hid.start()

    @pl.when(qb == steps - 1)
    def _():
        store_hid.wait()


def attention(doc_lengths, q_gain, k_gain, queries, kv, hidden):
    any_space = pl.BlockSpec(memory_space=pl.ANY)
    vmem = pltpu.VMEM
    f32, bf16 = jnp.float32, jnp.bfloat16
    return pl.pallas_call(
        attention_kernel,
        grid=(SHARD // BQ,),
        out_shape=(
            jax.ShapeDtypeStruct((SHARD, HEADS * HEAD), bf16),
            jax.ShapeDtypeStruct((TOK, MODEL), bf16),
        ),
        in_specs=[
            pl.BlockSpec(memory_space=pltpu.SMEM),
            pl.BlockSpec(memory_space=vmem),
            pl.BlockSpec(memory_space=vmem),
            pl.BlockSpec((BQ, HEADS * HEAD), lambda i: (i, 0)),
            pl.BlockSpec((2, 3 * SHARD, HEAD), lambda i: (0, 0, 0)),
            any_space,
        ],
        out_specs=(pl.BlockSpec((BQ, HEADS * HEAD), lambda i: (i, 0)), any_space),
        scratch_shapes=[
            vmem((HEAD, 3 * SHARD), bf16),
            vmem((HEADS * HEAD, BQ), bf16),
            vmem((HEADS, 3 * SHARD, BQ), f32),
            vmem((HEADS, 8, BQ), f32),
            vmem((HEADS, 8, BQ), f32),
            vmem((HEADS, HEAD, BQ), f32),
            vmem((BK, BQ), f32),
            vmem((TOK, MODEL), bf16),
            pltpu.SemaphoreType.DMA((2,)),
        ],
        compiler_params=pltpu.CompilerParams(vmem_limit_bytes=VMEM_LIMIT),
        name="attention",
    )(doc_lengths, q_gain, k_gain, queries, kv, hidden)


def per_device(
    residual, shared_out, expert_out, expert_id, gate_value, doc_lengths, norm_gain, w_query,
    key_value_weight, query_gain, key_gain,
):
    hidden, queries, kv = exchange(
        residual,
        shared_out,
        expert_out.reshape(N_EXP, SLOTS, MODEL),
        expert_id.reshape(1, TOK),
        gate_value.reshape(1, TOK),
        norm_gain,
        w_query,
        key_value_weight,
        query_gain.reshape(1, HEAD),
        key_gain.reshape(1, HEAD),
    )
    attended, hidden_out = attention(
        doc_lengths,
        query_gain.reshape(1, HEAD),
        key_gain.reshape(1, HEAD),
        queries.reshape(SHARD, HEADS * HEAD),
        kv.reshape(2, 3 * SHARD, HEAD),
        hidden,
    )
    return (hidden_out, attended)


def solution(mesh):
    placed = (
        P(("ctx", "exp"), None),
        P(("ctx", "exp"), None),
        P("ctx", "exp", None, None, None, None),
        P(("ctx", "exp"), None),
        P(("ctx", "exp"), None),
        P(),
        P(),
        P("ctx", "exp"),
        P("ctx", None),
        P(),
        P(),
    )
    return jax.shard_map(
        per_device,
        mesh=mesh,
        in_specs=placed,
        out_specs=(P(("ctx", "exp"), None), P("ctx", "exp")),
        check_vma=False,
    )
```
